128 devices in a mesh: drift: 16 (over z, y), cross: 8 (over x, core).
Axes of the slice: x: 4, y: 4, z: 4, core: 2. Of those that a mesh axis runs over, the one named last changes fastest.
Arguments:
- fluid_field: float32 [3, 32, 16, 1024], P(None, 'drift', 'cross'), may hold values from -6 to 6
- coords: float32 [3, 16, 8, 2048], P(None, 'drift', 'cross'), may hold values from -1 to 1
- velocity: float32 [3, 16, 8, 2048], P(None, 'drift', 'cross'), may hold values from -4 to 4
- drag_factor: float32 [16, 8, 2048], P('drift', 'cross'), may hold values from 0.05 to 0.5
- host_ids: int32 [16, 8, 2048], P('drift', 'cross'), may hold values from 0 to 7, as said below
- migrants: int32 [16, 8, 4, 512], P('drift', 'cross'), may hold values from -1 to 2047, as said below
Outputs:
- fluid_next: float32 [3, 32, 16, 1024], P(None, 'drift', 'cross')
- velocity_next: float32 [3, 16, 8, 2048], P(None, 'drift', 'cross')
The draws below stay inside these ranges and needn't reach their ends.
Inputs may be any that keep to these rules, and one draw needn't show every extreme that they name: `host_ids`: for a particle in list d of migrants the host element lies on the layer of the neighbour tile next to the particle's own tile: x = 1 for d = 0, x = 0 for d = 1, y = 1 for d = 2, y = 0 for d = 3. `migrants`: entry [tile, d] lists in ascending order the particles of that tile hosted by neighbour d (0: one lower along drift, 1: one higher along drift, 2: one lower across, 3: one higher across), then -1 padding. A particle stands in at most one list. Every tile has one full list of 512.
All inputs are finite; a program needn't handle non-finite values.
Results may differ from the reference program's by a relative error of at most 0.0003.
Values sent between devices are 32-bit elements; how exact they have to be, the bound alone decides.
No kernel may reach another device: no remote copies, remote signals or barrier semaphores. Data moves between devices by JAX's collectives and lax.ppermute only.
A program may use at most 64 MiB of HBM per device.

```python
import math
import jax
import jax.numpy as jnp
from jax import lax

TILE_X = 2
TILE_Y = 2
LAYERS = 2
PARTICLES = 2048
MIGRANTS = 512
GRID_X = 32
GRID_Y = 16
N_DRIFT = 16
N_CROSS = 8


def shuffle_one(shuffle_key):
    return jax.random.permutation(shuffle_key, PARTICLES).astype(jnp.int32)


def migrant_lists(key):
    key = jax.random.fold_in(key, 11)
    tile_count = N_DRIFT * N_CROSS
    shuffle_keys = jax.random.split(jax.random.fold_in(key, 1), tile_count)
    shuffled = jax.vmap(shuffle_one)(shuffle_keys)
    counts = jax.random.randint(jax.random.fold_in(key, 2), (tile_count, 4), MIGRANTS // 2, MIGRANTS + 1)
    fullest = jax.random.randint(jax.random.fold_in(key, 3), (tile_count,), 0, 4)
    counts = jnp.where(jnp.arange(4)[None, :] == fullest[:, None], MIGRANTS, counts)
    candidates = shuffled[:, :4 * MIGRANTS].reshape(tile_count, 4, MIGRANTS)
    usable = jnp.arange(MIGRANTS)[None, None, :] < counts[:, :, None]
    chosen = jnp.sort(jnp.where(usable, candidates, PARTICLES), axis=-1)
    return jnp.where(chosen == PARTICLES, -1, chosen).astype(jnp.int32)


def codes_one(migrant_rows):
    codes_out = jnp.zeros((PARTICLES,), jnp.int32)
    for direction in range(4):
        entries = migrant_rows[direction]
        targets = jnp.where(entries < 0, PARTICLES, entries)
        codes_out = codes_out.at[targets].set(direction + 1, mode='drop')
    return codes_out


def draw_migrants(key, part):
    lists_all = migrant_lists(key)
    return lists_all.reshape(N_DRIFT, N_CROSS, 4, MIGRANTS)


def draw_host_ids(key, part):
    lists_all = migrant_lists(key)
    key = jax.random.fold_in(key, 5)
    tile_count = N_DRIFT * N_CROSS
    hop = jax.vmap(codes_one)(lists_all)
    along_drift = jax.random.randint(jax.random.fold_in(key, 1), (tile_count, PARTICLES), 0, TILE_X)
    along_cross = jax.random.randint(jax.random.fold_in(key, 2), (tile_count, PARTICLES), 0, TILE_Y)
    along_depth = jax.random.randint(jax.random.fold_in(key, 3), (tile_count, PARTICLES), 0, LAYERS)
    along_drift = jnp.where(hop == 1, TILE_X - 1, jnp.where(hop == 2, 0, along_drift))
    along_cross = jnp.where(hop == 3, TILE_Y - 1, jnp.where(hop == 4, 0, along_cross))
    result = (along_drift * TILE_Y + along_cross) * LAYERS + along_depth
    return result.reshape(N_DRIFT, N_CROSS, PARTICLES).astype(jnp.int32)


def level_of(rng, shape, pieces, low, high):
    factor_of = 1.0
    for axis_at, blocks in pieces:
        steps = jax.random.uniform(jax.random.fold_in(jax.random.fold_in(rng, 6), axis_at), (blocks,), jnp.float32, low / len(pieces), high / len(pieces))
        factor_of = factor_of * jnp.repeat(jnp.exp(steps), shape[axis_at] // blocks).reshape((-1,) + (1,) * (len(shape) - 1 - axis_at))
    return factor_of


def bell_draw(own_key, shape, width, reach, cuts=(), held_as=jnp.bfloat16):
    drawn = jax.random.normal(own_key, shape, jnp.float32) * width
    if len(cuts) > 0:
        drawn = level_of(own_key, shape, cuts, -0.22, 0.18) * drawn
    return jnp.clip(drawn, min=-reach, max=reach).astype(held_as)


def setup_inputs(seed: int = 0) -> dict:
    key_of = jax.random.split(jax.random.key(seed), 7)
    fluid_field = bell_draw(key_of[0], (3, GRID_X, GRID_Y, LAYERS * 512), 1.0, 6.0, ((1, 16), (2, 8)), jnp.float32)
    coords = jnp.clip(jax.random.uniform(key_of[1], (3, N_DRIFT, N_CROSS, PARTICLES), jnp.float32, -1.0, 1.0) * level_of(key_of[1], (3, N_DRIFT, N_CROSS, PARTICLES), ((1, 16), (2, 8)), -0.4, 0.0), -1.0, 1.0)
    velocity = bell_draw(key_of[2], (3, N_DRIFT, N_CROSS, PARTICLES), 0.5, 4.0, ((1, 16), (2, 8)), jnp.float32)
    drag_factor = jnp.clip(jnp.exp(math.log(0.5) - 2.3025851 * jax.random.uniform(key_of[3], (N_DRIFT, N_CROSS, PARTICLES), jnp.float32) ** level_of(key_of[3], (N_DRIFT, N_CROSS, PARTICLES), ((0, 16), (1, 8)), -0.2, 0.2)), 0.05, 0.5)
    host_ids = draw_host_ids(jax.random.fold_in(key_of[6], 71), 0)
    migrants = draw_migrants(jax.random.fold_in(key_of[6], 71), 0)
    return {"fluid_field": fluid_field, "coords": coords, "velocity": velocity, "drag_factor": drag_factor, "host_ids": host_ids, "migrants": migrants}


mass_ratio = 4.0
diffusion_rate = 0.002
penalty_rate = 0.05


def node_points():
    counter = jnp.arange(8, dtype=jnp.float32)
    return -jnp.cos(jnp.pi * counter / 7.0)


def lagrange_weights(points):
    nodes_all = node_points()
    differ = points[:, None] - nodes_all[None, :]
    columns = []
    for target in range(8):
        numerator = jnp.ones_like(points)
        denominator = jnp.ones((), jnp.float32)
        for partner in range(8):
            if partner != target:
                numerator = numerator * differ[:, partner]
                denominator = denominator * (nodes_all[target] - nodes_all[partner])
        columns.append(numerator / denominator)
    return jnp.stack(columns, axis=1)


def node_weights(coords):
    weight_drift = lagrange_weights(coords[0])
    weight_cross = lagrange_weights(coords[1])
    weight_depth = lagrange_weights(coords[2])
    joined = weight_drift[:, :, None, None] * weight_cross[:, None, :, None] * weight_depth[:, None, None, :]
    return joined.reshape(-1, 512)


def couple_rows(element_table, coords, velocity, drag_factor, host_ids):
    usable = host_ids >= 0
    safe_rows = jnp.where(usable, host_ids, 0)
    weights = node_weights(coords)
    sampled = element_table[:, safe_rows, :]
    carried = jnp.sum(sampled * weights[None], axis=2)
    slip_speed = carried - velocity
    updated = velocity + drag_factor[None] * slip_speed
    reaction = jnp.where(usable[None], -mass_ratio * drag_factor[None] * slip_speed, 0.0)
    spread = reaction[:, :, None] * weights[None]
    return updated, spread, safe_rows


def hop_codes(migrant_rows, particle_count):
    codes_out = jnp.zeros((particle_count,), jnp.int32)
    for direction in range(4):
        entries = migrant_rows[direction]
        targets = jnp.where(entries < 0, particle_count, entries).astype(jnp.int32)
        codes_out = codes_out.at[targets].set(direction + 1, mode="drop")
    return codes_out


def second_derivative():
    nodes_all = node_points()
    row_index = jnp.arange(8)[:, None]
    column_index = jnp.arange(8)[None, :]
    end_scale = jnp.where((jnp.arange(8) == 0) | (jnp.arange(8) == 7), 2.0, 1.0).astype(jnp.float32)
    sign_table = jnp.where((row_index + column_index) % 2 == 0, 1.0, -1.0).astype(jnp.float32)
    node_gaps = nodes_all[:, None] - nodes_all[None, :] + jnp.eye(8, dtype=jnp.float32)
    off_diagonal = (end_scale[:, None] / end_scale[None, :]) * sign_table / node_gaps
    off_diagonal = jnp.where(row_index == column_index, 0.0, off_diagonal)
    derivative = off_diagonal - jnp.diag(jnp.sum(off_diagonal, axis=1))
    return jnp.dot(derivative, derivative, precision=lax.Precision.HIGHEST)


def interior(field_state):
    second = second_derivative()
    highest = lax.Precision.HIGHEST
    result = jnp.einsum("ia,...ajk->...ijk", second, field_state, precision=highest)
    result = result + jnp.einsum("jb,...ibk->...ijk", second, field_state, precision=highest)
    result = result + jnp.einsum("kc,...ijc->...ijk", second, field_state, precision=highest)
    return result


def face_terms(field_state, below_x, above_x, below_y, above_y):
    depth_low = field_state[..., 0]
    depth_high = field_state[..., 7]
    wall_zeros = jnp.zeros_like(depth_low[:, :, :, :1])
    below_z = jnp.concatenate([wall_zeros, depth_high[:, :, :, :-1]], axis=3)
    above_z = jnp.concatenate([depth_low[:, :, :, 1:], wall_zeros], axis=3)
    face_sum = jnp.zeros_like(field_state)
    face_sum = face_sum.at[..., 0, :, :].add(below_x - field_state[..., 0, :, :])
    face_sum = face_sum.at[..., 7, :, :].add(above_x - field_state[..., 7, :, :])
    face_sum = face_sum.at[..., :, 0, :].add(below_y - field_state[..., :, 0, :])
    face_sum = face_sum.at[..., :, 7, :].add(above_y - field_state[..., :, 7, :])
    face_sum = face_sum.at[..., 0].add(below_z - depth_low)
    face_sum = face_sum.at[..., 7].add(above_z - depth_high)
    return face_sum


def reference(fluid_field, coords, velocity, drag_factor, host_ids, migrants):
    tile_count = N_DRIFT * N_CROSS
    element_table = fluid_field.reshape(3, GRID_X * GRID_Y * LAYERS, 512)
    tile_coords_all = coords.reshape(3, tile_count, PARTICLES).transpose(1, 0, 2)
    tile_velocity_all = velocity.reshape(3, tile_count, PARTICLES).transpose(1, 0, 2)
    tile_drag_all = drag_factor.reshape(tile_count, PARTICLES)
    tile_hosts_all = host_ids.reshape(tile_count, PARTICLES)
    tile_lists_all = migrants.reshape(tile_count, 4, MIGRANTS)
    tile_numbers = jnp.arange(tile_count, dtype=jnp.int32)
    drift_numbers = tile_numbers // N_CROSS
    cross_numbers = tile_numbers % N_CROSS

    def per_tile(deposit, inputs):
        tile_coords, tile_velocity, tile_drag, tile_hosts, tile_lists, drift_index, cross_index = inputs
        hop = hop_codes(tile_lists, PARTICLES)
        along_drift = tile_hosts // (TILE_Y * LAYERS)
        along_cross = (tile_hosts // LAYERS) % TILE_Y
        along_depth = tile_hosts % LAYERS
        drift_move = jnp.where(hop == 1, -1, jnp.where(hop == 2, 1, 0))
        cross_move = jnp.where(hop == 3, -1, jnp.where(hop == 4, 1, 0))
        owner_drift = (drift_index + drift_move) % N_DRIFT
        owner_cross = (cross_index + cross_move) % N_CROSS
        global_x = owner_drift * TILE_X + along_drift
        global_y = owner_cross * TILE_Y + along_cross
        global_ids = ((global_x * GRID_Y + global_y) * LAYERS + along_depth).astype(jnp.int32)
        updated, spread, safe_rows = couple_rows(element_table, tile_coords, tile_velocity, tile_drag, global_ids)
        deposit = deposit.at[:, safe_rows, :].add(spread)
        return deposit, updated

    start = jnp.zeros((3, GRID_X * GRID_Y * LAYERS, 512), jnp.float32)
    deposit, updated_all = lax.scan(per_tile, start, (tile_coords_all, tile_velocity_all, tile_drag_all, tile_hosts_all, tile_lists_all, drift_numbers, cross_numbers))
    velocity_next = updated_all.transpose(1, 0, 2).reshape(3, N_DRIFT, N_CROSS, PARTICLES)

    deposit_grid = deposit.reshape(3, GRID_X, GRID_Y, LAYERS, 8, 8, 8)
    field_state = fluid_field.reshape(3, GRID_X, GRID_Y, LAYERS, 8, 8, 8)
    for substep in range(2):
        below_x = jnp.roll(field_state[..., 7, :, :], 1, axis=1)
        above_x = jnp.roll(field_state[..., 0, :, :], -1, axis=1)
        below_y = jnp.roll(field_state[..., :, 7, :], 1, axis=2)
        above_y = jnp.roll(field_state[..., :, 0, :], -1, axis=2)
        rate_now = diffusion_rate * interior(field_state) + penalty_rate * face_terms(field_state, below_x, above_x, below_y, above_y)
        field_state = field_state + rate_now + 0.5 * deposit_grid
    fluid_next = field_state.reshape(3, GRID_X, GRID_Y, LAYERS * 512)
    return fluid_next, velocity_next
```

```python
import functools

import jax
import jax.numpy as jnp
import numpy as np
from jax import lax
from jax.experimental import pallas as pl
from jax.experimental.pallas import tpu as pltpu
from jax.sharding import PartitionSpec as P


F32 = jnp.float32
BF16 = jnp.bfloat16
MASS = 4.0
DIFF = 0.002
PEN = 0.05
VMEM = 24 << 20

NODES = -np.cos(np.pi * np.arange(8) / 7.0)
DENOM = np.array([np.prod([NODES[t] - NODES[m] for m in range(8) if m != t]) for t in range(8)])


def second_np():
    end = np.where((np.arange(8) == 0) | (np.arange(8) == 7), 2.0, 1.0)
    d = np.zeros((8, 8))
    for i in range(8):
        for m in range(8):
            if i != m:
                d[i, m] = end[i] / end[m] * (-1.0) ** (i + m) / (NODES[i] - NODES[m])
    d -= np.diag(d.sum(axis=1))
    return d @ d


def operator_tables():
    s = second_np()
    tab = np.zeros((2, 4, 8, 128))
    a1 = np.arange(128) // 64
    b = np.arange(128) // 8 % 8
    k = np.arange(128) % 8
    for sub in range(8):
        a2 = sub // 2
        a = 2 * a2 + a1
        for step in range(4):
            other = (a2 - step) % 4
            tab[0, step, sub] = DIFF * s[a, 2 * other + a1]
            tab[1, step, sub] = DIFF * s[a, 2 * other + 1 - a1]
        mult = ((a == 0) | (a == 7)) * 1.0 + ((b == 0) | (b == 7)) + ((k == 0) | (k == 7))
        tab[0, 0, sub] += 1.0 - PEN * mult
    eye = np.eye(8)
    side = DIFF * (np.kron(s, eye) + np.kron(eye, s))
    lane = np.kron(np.eye(2), side).T.astype(np.float32)
    hi = lane.astype(jnp.bfloat16)
    lo = (lane - hi.astype(np.float32)).astype(jnp.bfloat16)
    half = np.concatenate([hi, lo], axis=1)
    return tab.reshape(64, 128).astype(np.float32), np.concatenate([half, half], axis=0)


def iota(shape, dim):
    return lax.broadcasted_iota(jnp.int32, shape, dim)


def split(x):
    hi = x.astype(BF16)
    lo = (x - hi.astype(F32)).astype(BF16)
    return hi, lo


def row_of(ref, r):
    return jnp.broadcast_to(ref[r : r + 1, :], (8, 128))


def sublane_table(values):
    sub = iota((8, 128), 0)
    out = jnp.full((8, 128), float(values[0]), F32)
    for i in range(1, 8):
        out = jnp.where(sub == i, float(values[i]), out)
    return out


def node_tables(order):
    partners = [[m for m in range(8) if m != t] for t in order]
    tables = [sublane_table([NODES[p[j]] for p in partners]) for j in range(7)]
    return tables, sublane_table([1.0 / DENOM[t] for t in order])


def lagrange(s, tables):
    nodes, scale = tables
    out = (s - nodes[0]) * scale
    for t in nodes[1:]:
        out = out * (s - t)
    return out


def tile_of(ref, c, x, z):
    r = ((c * 2 + x) * 2 + z) * 8
    return ref[r : r + 8, :]


CXZ = [(c, x, z) for c in range(3) for x in range(2) for z in range(2)]


def parity(axis):
    return lax.rem(lax.axis_index(axis), 2) == 1


def face_masks():
    sub, lane = iota((8, 128), 0), iota((8, 128), 1)
    a2, y, a1, b, k = sub // 2, sub % 2, lane // 64, lane // 8 % 8, lane % 8
    pick = lambda cond: jnp.where(cond, PEN, 0.0).astype(F32)
    return dict(
        x_lo=pick((a2 == 0) & (a1 == 0)),
        x_hi=pick((a2 == 3) & (a1 == 1)),
        y_lo=pick((y == 0) & (b == 0)),
        y_hi=pick((y == 1) & (b == 7)),
        y_in_hi=pick((y == 0) & (b == 7)),
        y_in_lo=pick((y == 1) & (b == 0)),
        z_lo=pick(k == 0),
        z_hi=pick(k == 7),
    )


def pack_faces(get):
    lane = iota((8, 128), 1)
    b = lane // 8 % 8
    low = [get(c, 0, z)[0:2] for c in range(3) for z in range(2)]
    high = [get(c, 1, z)[6:8] for c in range(3) for z in range(2)]
    fill = jnp.zeros((4, 128), F32)
    x_lo = pltpu.roll(jnp.concatenate(low + [fill], axis=0), 64, 1)
    x_hi = pltpu.roll(jnp.concatenate(high + [fill], axis=0), 64, 1)
    y_lo, y_hi = [], []
    for group in range(2):
        lo = hi = None
        for i in range(6):
            v = get(*CXZ[group * 6 + i])
            here = b == i
            to_lo = v if i == 0 else pltpu.roll(v, 8 * i, 1)
            to_hi = pltpu.roll(v, (8 * i + 72) % 128, 1)
            lo = to_lo if lo is None else jnp.where(here, to_lo, lo)
            hi = to_hi if hi is None else jnp.where(here, to_hi, hi)
        y_lo.append(pltpu.roll(lo, 1, 0))
        y_hi.append(pltpu.roll(hi, 7, 0))
    return x_lo, x_hi, jnp.concatenate(y_lo, axis=0), jnp.concatenate(y_hi, axis=0)


def received_faces(odd_d, odd_c, drift_odd, drift_even, cross_odd, cross_even):
    m = face_masks()
    from_hi_x = jnp.where(odd_d, drift_odd, drift_even)
    from_lo_x = jnp.where(odd_d, drift_even, drift_odd)
    from_hi_y = jnp.where(odd_c, cross_odd, cross_even)
    from_lo_y = jnp.where(odd_c, cross_even, cross_odd)
    hi_y = [pltpu.roll(from_hi_y[8 * g : 8 * g + 8], 56, 1) for g in range(2)]
    lo_y = [from_lo_y[8 * g : 8 * g + 8] for g in range(2)]

    def at(c, x, z):
        r = 2 * (c * 2 + z)
        rows = (from_hi_x if x == 1 else from_lo_x)[r : r + 2]
        out = jnp.concatenate([rows] * 4, axis=0) * (m["x_hi"] if x == 1 else m["x_lo"])
        index = (c * 2 + x) * 2 + z
        g, i = index // 6, index % 6
        back = (128 - 8 * i) % 128
        hi = pltpu.roll(hi_y[g], back, 1) if back else hi_y[g]
        lo = pltpu.roll(lo_y[g], back, 1) if back else lo_y[g]
        return out + hi * m["y_hi"] + lo * m["y_lo"]

    return at


def local_step(get, tab, lane_op):
    m = face_masks()
    whole = jnp.concatenate([get(*i) for i in CXZ], axis=0)
    hi, lo = split(whole)
    product = jnp.dot(jnp.concatenate([hi, lo], axis=1), lane_op[...], preferred_element_type=F32)
    product = product[:, 0:128] + product[:, 128:256]
    turned = {}
    for i in CXZ:
        v = get(*i)
        w = pltpu.roll(v, 64, 1)
        turned[i] = (
            [v] + [pltpu.roll(v, 2 * s, 0) for s in range(1, 4)],
            [w] + [pltpu.roll(w, 2 * s, 0) for s in range(1, 4)],
        )
    out = {}
    for n, (c, x, z) in enumerate(CXZ):
        v = turned[c, x, z][0][0]
        total = product[8 * n : 8 * n + 8]
        for kind in range(2):
            for s in range(4):
                r = (kind * 4 + s) * 8
                total = total + turned[c, x, z][kind][s] * tab[r : r + 8, :]
        beside = turned[c, 1 - x, z][1]
        total = total + (beside[3] * m["x_hi"] if x == 0 else beside[1] * m["x_lo"])
        total = total + pltpu.roll(pltpu.roll(v, 56, 1), 7, 0) * m["y_in_hi"]
        total = total + pltpu.roll(pltpu.roll(v, 72, 1), 1, 0) * m["y_in_lo"]
        across = turned[c, x, 1 - z][0][0]
        if z == 0:
            total = total + pltpu.roll(across, 7, 1) * m["z_hi"]
        else:
            total = total + pltpu.roll(across, 121, 1) * m["z_lo"]
        out[c, x, z] = total
    return out


def field_operand(get):
    lane = iota((96, 128), 1)
    whole = jnp.concatenate([get(*i) for i in CXZ], axis=0)
    hi = whole.astype(BF16).astype(F32)
    lo = whole - hi
    first = jnp.where(lane < 64, hi, pltpu.roll(lo, 64, 1)).astype(BF16)
    second = jnp.where(lane < 64, pltpu.roll(hi, 64, 1), lo).astype(BF16)
    rows = jnp.concatenate([first, second], axis=0)
    return jnp.concatenate([rows, rows], axis=1)


def couple(n_tiles, coords_at, velocity_at, drag_at, host_at, field, emit, base, wts, ra, group=4):
    even = node_tables([0, 0, 2, 2, 4, 4, 6, 6])
    odd = node_tables([1, 1, 3, 3, 5, 5, 7, 7])
    plain = node_tables(list(range(8)))
    y_sub = iota((8, 128), 0) % 2
    total = None
    for g in range(n_tiles // group):
        for t in range(g * group, g * group + group):
            cols = slice(128 * t, 128 * t + 128)
            sx, sy, sz = coords_at(t)
            y_of = (host_at(t) // 2) % 2
            keep = y_of == y_sub
            base[0:8, cols] = jnp.where(keep, lagrange(sx, even), 0.0)
            base[8:16, cols] = jnp.where(keep, lagrange(sx, odd), 0.0)
            lb, lc = lagrange(sy, plain), lagrange(sz, plain)
            w = jnp.concatenate([jnp.broadcast_to(lb[b : b + 1], (8, 128)) * lc for b in range(8)], axis=0)
            hi, lo = split(w)
            wts[0:64, cols] = hi
            wts[64:128, cols] = hi
            wts[128:192, cols] = lo
            wts[192:256, cols] = lo
        span = slice(128 * g * group, 128 * (g + 1) * group)
        h = jnp.dot(field, wts[:, span], preferred_element_type=F32)
        for t in range(g * group, g * group + group):
            cols = slice(128 * t, 128 * t + 128)
            sub = slice(128 * (t - g * group), 128 * (t - g * group) + 128)
            code = host_at(t)
            q = (code // 4) * 2 + code % 2
            drag = drag_at(t) * (-MASS)
            at = [q == i for i in range(4)]
            lines = [base[0:8, cols], base[8:16, cols]]
            carried = []
            for c in range(3):
                acc = None
                for a1 in range(2):
                    r = (a1 * 12 + c * 4) * 8
                    v = h[r : r + 8, sub]
                    for i in range(1, 4):
                        v = jnp.where(at[i], h[r + 8 * i : r + 8 * i + 8, sub], v)
                    v = v * lines[a1]
                    acc = v if acc is None else acc + v
                carried.append(jnp.sum(acc, axis=0, keepdims=True))
            emit(t, carried)
            speed = velocity_at(t)
            for c in range(3):
                r = drag * (carried[c] - speed[c])
                for a1 in range(2):
                    v = r * lines[a1]
                    hi = v.astype(BF16).astype(F32)
                    lo = v - hi
                    for part, value in enumerate((hi, lo)):
                        first = ((part * 2 + a1) * 3 + c) * 32
                        rows = jnp.concatenate([jnp.where(at[i], value, 0.0) for i in range(4)], axis=0)
                        ra[first : first + 32, cols] = rows.astype(BF16)
        d = lax.dot_general(
            ra[:, span], wts[64:192, span], (((1,), (1,)), ((), ())), preferred_element_type=F32
        )
        total = d if total is None else total + d
    d = total[0:192] + total[192:384]
    d = d + pltpu.roll(d, 64, 1)
    return jnp.where(iota((96, 128), 1) < 64, d[0:96], d[96:192])


def lists_onehot(mig, store):
    high = []
    lane_row = iota((128, 128), 0)
    for t in range(16):
        idx = mig[t : t + 1, :]
        store[:, 128 * t : 128 * t + 128] = jnp.where(lane_row == (idx & 127), 1.0, 0.0).astype(BF16)
        high.append(idx >> 7)
    return high


def send_kernel(fl, co, ve, dr, ho, mi, o0, o1, o2, o3, vf, vc, vv, vd, vh, vm, table, onehot, sems):
    copies = [
        pltpu.make_async_copy(src, dst, sems.at[n])
        for n, (src, dst) in enumerate(((mi, vm), (co, vc), (ve, vv), (dr, vd), (ho, vh), (fl, vf)))
    ]
    for copy in copies:
        copy.start()
    copies[0].wait()
    high = lists_onehot(vm, onehot)
    for copy in copies[1:]:
        copy.wait()
    for c in range(3):
        table[pl.ds(c, 16, stride=8), :] = vc[16 * c : 16 * c + 16, :]
        table[pl.ds(3 + c, 16, stride=8), :] = vv[16 * c : 16 * c + 16, :]
    table[pl.ds(6, 16, stride=8), :] = vd[...]
    table[pl.ds(7, 16, stride=8), :] = vh[...].astype(F32)
    hi, lo = split(table[...])
    hi_lo = jnp.concatenate([hi, lo], axis=1)
    odd_d, odd_c = parity("drift"), parity("cross")
    x_lo, x_hi, y_lo, y_hi = pack_faces(functools.partial(tile_of, vf))
    o0[32:48, :] = jnp.where(odd_d, x_hi, x_lo)
    o1[32:48, :] = jnp.where(odd_d, x_lo, x_hi)
    o2[32:48, :] = jnp.where(odd_c, y_hi, y_lo)
    o3[32:48, :] = jnp.where(odd_c, y_lo, y_hi)
    for t in range(4):
        span = onehot[:, 512 * t : 512 * t + 512]
        y = jnp.dot(hi_lo, jnp.concatenate([span, span], axis=0), preferred_element_type=F32)
        found = []
        for d in range(4):
            h = high[4 * t + d]
            g = jnp.zeros((8, 128), F32)
            for row in range(16):
                g = jnp.where(h == row, y[8 * row : 8 * row + 8, 128 * d : 128 * d + 128], g)
            found.append(g)
        rows = slice(8 * t, 8 * t + 8)
        o0[rows, :] = jnp.where(odd_d, found[1], found[0])
        o1[rows, :] = jnp.where(odd_d, found[0], found[1])
        o2[rows, :] = jnp.where(odd_c, found[3], found[2])
        o3[rows, :] = jnp.where(odd_c, found[2], found[3])


def own_kernel(fl, co, ve, dr, ho, mi, tab, lane_op, dep_out, vel_out, base_out, operand_out, onehot, car, base, wts, ra):
    high = lists_onehot(mi, onehot)
    sub16 = iota((16, 128), 0)
    rows = jnp.concatenate([jnp.where(h == sub16, 1.0, 0.0) for h in high], axis=1).astype(BF16)
    listed = lax.dot_general(rows, onehot[...], (((1,), (1,)), ((), ())), preferred_element_type=F32)
    own = jnp.where(listed > 0.5, 0.0, 1.0)
    get = functools.partial(tile_of, fl)
    field = field_operand(get)
    operand_out[...] = field
    drag_own = dr[...] * own

    def emit(t, carried):
        for c in range(3):
            car[16 * c + t : 16 * c + t + 1, :] = carried[c]

    dep_out[...] = couple(
        16,
        lambda t: [row_of(co, 16 * c + t) for c in range(3)],
        lambda t: [row_of(ve, 16 * c + t) for c in range(3)],
        lambda t: jnp.broadcast_to(drag_own[t : t + 1], (8, 128)),
        lambda t: row_of(ho, t),
        field, emit, base, wts, ra,
    )
    for c in range(3):
        r = slice(16 * c, 16 * c + 16)
        vel_out[r, :] = ve[r, :] + dr[...] * (car[r, :] * own - ve[r, :])
    out = local_step(get, tab, lane_op)
    for n, i in enumerate(CXZ):
        base_out[8 * n : 8 * n + 8, :] = out[i]


def host_kernel(r0, r1, r2, r3, operand, dep_in, base_in, u_out, dep_out, o0, o1, o2, o3, base, wts, ra):
    received, sent = (r0, r1, r2, r3), (o0, o1, o2, o3)
    odd_d, odd_c = parity("drift"), parity("cross")
    pick = lambda t, v: row_of(received[t // 4], 8 * (t % 4) + v)

    def emit(t, carried):
        for c in range(3):
            sent[t // 4][4 * (t % 4) + c : 4 * (t % 4) + c + 1, :] = carried[c]
        sent[t // 4][4 * (t % 4) + 3 : 4 * (t % 4) + 4, :] = carried[0]

    dep = dep_in[...] + couple(
        16,
        lambda t: [pick(t, c) for c in range(3)],
        lambda t: [pick(t, 3 + c) for c in range(3)],
        lambda t: pick(t, 6),
        lambda t: pick(t, 7).astype(jnp.int32),
        operand[...], emit, base, wts, ra,
    )
    dep_out[...] = dep
    faces = received_faces(odd_d, odd_c, *[r[32:48, :] for r in received])
    new = {}
    for n, i in enumerate(CXZ):
        r = slice(8 * n, 8 * n + 8)
        new[i] = base_in[r, :] + faces(*i) + 0.5 * dep[r]
        u_out[r, :] = new[i]
    x_lo, x_hi, y_lo, y_hi = pack_faces(lambda c, x, z: new[c, x, z])
    o0[16:32, :] = jnp.where(odd_d, x_hi, x_lo)
    o1[16:32, :] = jnp.where(odd_d, x_lo, x_hi)
    o2[16:32, :] = jnp.where(odd_c, y_hi, y_lo)
    o3[16:32, :] = jnp.where(odd_c, y_lo, y_hi)


def second_kernel(u, dep, tab, lane_op, out_ref):
    out = local_step(functools.partial(tile_of, u), tab, lane_op)
    for n, i in enumerate(CXZ):
        r = slice(8 * n, 8 * n + 8)
        out_ref[r, :] = out[i] + 0.5 * dep[r, :]


def last_kernel(r0, r1, r2, r3, base, vel, dr, mi, onehot, fluid_out, vel_out):
    odd_d, odd_c = parity("drift"), parity("cross")
    faces = received_faces(odd_d, odd_c, *[r[16:32, :] for r in (r0, r1, r2, r3)])
    for n, i in enumerate(CXZ):
        r = slice(8 * n, 8 * n + 8)
        fluid_out[r, :] = base[r, :] + faces(*i)
    sub16 = iota((16, 128), 0)
    columns = []
    for t in range(4):
        rows = slice(4 * t, 4 * t + 4)
        back = [
            jnp.where(odd_d, r1[rows, :], r0[rows, :]),
            jnp.where(odd_d, r0[rows, :], r1[rows, :]),
            jnp.where(odd_c, r3[rows, :], r2[rows, :]),
            jnp.where(odd_c, r2[rows, :], r3[rows, :]),
        ]
        for d in range(4):
            at = (mi[4 * t + d : 4 * t + d + 1, :] >> 7) == sub16
            columns.append(jnp.concatenate([jnp.where(at, back[d][c : c + 1], 0.0) for c in range(3)], axis=0))
    hi, lo = split(jnp.concatenate(columns, axis=1))
    put = lax.dot_general(
        jnp.concatenate([hi, lo], axis=0), onehot[...], (((1,), (1,)), ((), ())), preferred_element_type=F32
    )
    put = put[0:48] + put[48:96]
    for c in range(3):
        r = slice(16 * c, 16 * c + 16)
        vel_out[r, :] = vel[r, :] + dr[...] * put[r]


def shape(rows, dtype=F32, lanes=128):
    return jax.ShapeDtypeStruct((rows, lanes), dtype)


def call(kernel, outs, scratch=(), in_specs=None, cost=0, **kw):
    if in_specs is not None:
        kw["in_specs"] = in_specs
    return pl.pallas_call(
        kernel,
        out_shape=outs,
        scratch_shapes=list(scratch),
        cost_estimate=pl.CostEstimate(flops=cost, bytes_accessed=0, transcendentals=0),
        compiler_params=pltpu.CompilerParams(vmem_limit_bytes=VMEM),
        **kw,
    )


def swap(block, axis, odd):
    count = lax.axis_size(axis)
    pairs = []
    for i in range(odd, count + odd, 2):
        first, other = i % count, (i + 1) % count
        pairs += [(first, other), (other, first)]
    return lax.ppermute(block, axis, pairs)


def exchange(blocks):
    order = (("drift", 1), ("drift", 0), ("cross", 1), ("cross", 0))
    return [swap(block, axis, odd) for block, (axis, odd) in zip(blocks, order)]


def per_device(fluid_field, coords, velocity, drag_factor, host_ids, migrants):
    field = fluid_field.reshape(3, 2, 2, 8, 128).transpose(0, 1, 3, 2, 4).reshape(96, 128)
    args = (
        field,
        coords.reshape(48, 128),
        velocity.reshape(48, 128),
        drag_factor.reshape(16, 128),
        host_ids.reshape(16, 128),
        migrants.reshape(4, 4, 128).transpose(1, 0, 2).reshape(16, 128),
    )
    tab, lane_op = (jnp.asarray(t) for t in operator_tables())
    couple_scratch = [pltpu.VMEM((16, 2048), F32), pltpu.VMEM((256, 2048), BF16), pltpu.VMEM((384, 2048), BF16)]
    sends = call(
        send_kernel,
        [shape(48)] * 4,
        [pltpu.VMEM(a.shape, a.dtype) for a in args]
        + [pltpu.VMEM((128, 128), F32), pltpu.VMEM((128, 2048), BF16), pltpu.SemaphoreType.DMA((6,))],
        in_specs=[pl.BlockSpec(memory_space=pl.ANY)] * 6,
    )(*args)
    received = exchange(sends)
    dep, vel, base, operand, onehot = call(
        own_kernel,
        [shape(96), shape(48), shape(96), shape(192, BF16, 256), shape(128, BF16, 2048)],
        [pltpu.VMEM((48, 128), F32)] + couple_scratch,
        cost=1 << 31,
    )(*args, tab, lane_op)
    u, dep, *sends = call(host_kernel, [shape(96)] * 2 + [shape(32)] * 4, couple_scratch)(
        *received, operand, dep, base
    )
    received = exchange(sends)
    base = call(second_kernel, shape(96), cost=1 << 30)(u, dep, tab, lane_op)
    fluid, vel = call(last_kernel, [shape(96), shape(48)])(*received, base, vel, args[3], args[5], onehot)
    fluid = fluid.reshape(3, 2, 8, 2, 128).transpose(0, 1, 3, 2, 4).reshape(3, 2, 2, 1024)
    return fluid, vel.reshape(3, 1, 1, 2048)


def solution(mesh):
    field = P(None, "drift", "cross", None)
    scalar = P("drift", "cross", None)
    return jax.shard_map(
        per_device,
        mesh=mesh,
        in_specs=(field, field, field, scalar, scalar, P("drift", "cross", None, None)),
        out_specs=(field, field),
        check_vma=False,
    )
```

```python
import functools

import jax
import jax.numpy as jnp
import numpy as np
from jax import lax
from jax.experimental import pallas as pl
from jax.experimental.pallas import tpu as pltpu
from jax.sharding import PartitionSpec as P


F32 = jnp.float32
BF16 = jnp.bfloat16
MASS = 4.0
DIFF = 0.002
PEN = 0.05
VMEM = 24 << 20

NODES = -np.cos(np.pi * np.arange(8) / 7.0)
DENOM = np.array([np.prod([NODES[t] - NODES[m] for m in range(8) if m != t]) for t in range(8)])


def second_np():
    end = np.where((np.arange(8) == 0) | (np.arange(8) == 7), 2.0, 1.0)
    d = np.zeros((8, 8))
    for i in range(8):
        for m in range(8):
            if i != m:
                d[i, m] = end[i] / end[m] * (-1.0) ** (i + m) / (NODES[i] - NODES[m])
    d -= np.diag(d.sum(axis=1))
    return d @ d


def operator_tables():
    s = second_np()
    tab = np.zeros((2, 4, 8, 128))
    a1 = np.arange(128) // 64
    b = np.arange(128) // 8 % 8
    k = np.arange(128) % 8
    for sub in range(8):
        a2 = sub // 2
        a = 2 * a2 + a1
        for step in range(4):
            other = (a2 - step) % 4
            tab[0, step, sub] = DIFF * s[a, 2 * other + a1]
            tab[1, step, sub] = DIFF * s[a, 2 * other + 1 - a1]
        mult = ((a == 0) | (a == 7)) * 1.0 + ((b == 0) | (b == 7)) + ((k == 0) | (k == 7))
        tab[0, 0, sub] += 1.0 - PEN * mult
    eye = np.eye(8)
    side = DIFF * (np.kron(s, eye) + np.kron(eye, s))
    lane = np.kron(np.eye(2), side).T.astype(np.float32)
    hi = lane.astype(jnp.bfloat16)
    lo = (lane - hi.astype(np.float32)).astype(jnp.bfloat16)
    half = np.concatenate([hi, lo], axis=1)
    return tab.reshape(64, 128).astype(np.float32), np.concatenate([half, half], axis=0)


def iota(shape, dim):
    return lax.broadcasted_iota(jnp.int32, shape, dim)


def split(x):
    hi = x.astype(BF16)
    lo = (x - hi.astype(F32)).astype(BF16)
    return hi, lo


def row_of(ref, r):
    return jnp.broadcast_to(ref[r : r + 1, :], (8, 128))


def sublane_table(values):
    sub = iota((8, 128), 0)
    out = jnp.full((8, 128), float(values[0]), F32)
    for i in range(1, 8):
        out = jnp.where(sub == i, float(values[i]), out)
    return out


def node_tables(order):
    partners = [[m for m in range(8) if m != t] for t in order]
    tables = [sublane_table([NODES[p[j]] for p in partners]) for j in range(7)]
    return tables, sublane_table([1.0 / DENOM[t] for t in order])


def lagrange(s, tables):
    nodes, scale = tables
    out = (s - nodes[0]) * scale
    for t in nodes[1:]:
        out = out * (s - t)
    return out


def tile_of(ref, c, x, z):
    r = ((c * 2 + x) * 2 + z) * 8
    return ref[r : r + 8, :]


CXZ = [(c, x, z) for c in range(3) for x in range(2) for z in range(2)]


def parity(axis):
    return lax.rem(lax.axis_index(axis), 2) == 1


def face_masks():
    sub, lane = iota((8, 128), 0), iota((8, 128), 1)
    a2, y, a1, b, k = sub // 2, sub % 2, lane // 64, lane // 8 % 8, lane % 8
    pick = lambda cond: jnp.where(cond, PEN, 0.0).astype(F32)
    return dict(
        x_lo=pick((a2 == 0) & (a1 == 0)),
        x_hi=pick((a2 == 3) & (a1 == 1)),
        y_lo=pick((y == 0) & (b == 0)),
        y_hi=pick((y == 1) & (b == 7)),
        y_in_hi=pick((y == 0) & (b == 7)),
        y_in_lo=pick((y == 1) & (b == 0)),
        z_lo=pick(k == 0),
        z_hi=pick(k == 7),
    )


def pack_faces(get):
    lane = iota((8, 128), 1)
    b = lane // 8 % 8
    low = [get(c, 0, z)[0:2] for c in range(3) for z in range(2)]
    high = [get(c, 1, z)[6:8] for c in range(3) for z in range(2)]
    fill = jnp.zeros((4, 128), F32)
    x_lo = pltpu.roll(jnp.concatenate(low + [fill], axis=0), 64, 1)
    x_hi = pltpu.roll(jnp.concatenate(high + [fill], axis=0), 64, 1)
    y_lo, y_hi = [], []
    for group in range(2):
        lo = hi = None
        for i in range(6):
            v = get(*CXZ[group * 6 + i])
            here = b == i
            to_lo = v if i == 0 else pltpu.roll(v, 8 * i, 1)
            to_hi = pltpu.roll(v, (8 * i + 72) % 128, 1)
            lo = to_lo if lo is None else jnp.where(here, to_lo, lo)
            hi = to_hi if hi is None else jnp.where(here, to_hi, hi)
        y_lo.append(pltpu.roll(lo, 1, 0))
        y_hi.append(pltpu.roll(hi, 7, 0))
    return x_lo, x_hi, jnp.concatenate(y_lo, axis=0), jnp.concatenate(y_hi, axis=0)


def received_faces(odd_d, odd_c, drift_odd, drift_even, cross_odd, cross_even):
    m = face_masks()
    from_hi_x = jnp.where(odd_d, drift_odd, drift_even)
    from_lo_x = jnp.where(odd_d, drift_even, drift_odd)
    from_hi_y = jnp.where(odd_c, cross_odd, cross_even)
    from_lo_y = jnp.where(odd_c, cross_even, cross_odd)
    hi_y = [pltpu.roll(from_hi_y[8 * g : 8 * g + 8], 56, 1) for g in range(2)]
    lo_y = [from_lo_y[8 * g : 8 * g + 8] for g in range(2)]

    def at(c, x, z):
        r = 2 * (c * 2 + z)
        rows = (from_hi_x if x == 1 else from_lo_x)[r : r + 2]
        out = jnp.concatenate([rows] * 4, axis=0) * (m["x_hi"] if x == 1 else m["x_lo"])
        index = (c * 2 + x) * 2 + z
        g, i = index // 6, index % 6
        back = (128 - 8 * i) % 128
        hi = pltpu.roll(hi_y[g], back, 1) if back else hi_y[g]
        lo = pltpu.roll(lo_y[g], back, 1) if back else lo_y[g]
        return out + hi * m["y_hi"] + lo * m["y_lo"]

    return at


def local_step(get, tab, lane_op):
    m = face_masks()
    whole = jnp.concatenate([get(*i) for i in CXZ], axis=0)
    hi, lo = split(whole)
    product = jnp.dot(jnp.concatenate([hi, lo], axis=1), lane_op[...], preferred_element_type=F32)
    product = product[:, 0:128] + product[:, 128:256]
    turned = {}
    for i in CXZ:
        v = get(*i)
        w = pltpu.roll(v, 64, 1)
        turned[i] = (
            [v] + [pltpu.roll(v, 2 * s, 0) for s in range(1, 4)],
            [w] + [pltpu.roll(w, 2 * s, 0) for s in range(1, 4)],
        )
    out = {}
    for n, (c, x, z) in enumerate(CXZ):
        v = turned[c, x, z][0][0]
        total = product[8 * n : 8 * n + 8]
        for kind in range(2):
            for s in range(4):
                r = (kind * 4 + s) * 8
                total = total + turned[c, x, z][kind][s] * tab[r : r + 8, :]
        beside = turned[c, 1 - x, z][1]
        total = total + (beside[3] * m["x_hi"] if x == 0 else beside[1] * m["x_lo"])
        total = total + pltpu.roll(pltpu.roll(v, 56, 1), 7, 0) * m["y_in_hi"]
        total = total + pltpu.roll(pltpu.roll(v, 72, 1), 1, 0) * m["y_in_lo"]
        across = turned[c, x, 1 - z][0][0]
        if z == 0:
            total = total + pltpu.roll(across, 7, 1) * m["z_hi"]
        else:
            total = total + pltpu.roll(across, 121, 1) * m["z_lo"]
        out[c, x, z] = total
    return out


def field_operand(get):
    lane = iota((96, 128), 1)
    whole = jnp.concatenate([get(*i) for i in CXZ], axis=0)
    hi = whole.astype(BF16).astype(F32)
    lo = whole - hi
    first = jnp.where(lane < 64, hi, pltpu.roll(lo, 64, 1)).astype(BF16)
    second = jnp.where(lane < 64, pltpu.roll(hi, 64, 1), lo).astype(BF16)
    rows = jnp.concatenate([first, second], axis=0)
    return jnp.concatenate([rows, rows], axis=1)


def couple(n_tiles, coords_at, velocity_at, drag_at, host_at, field, emit, base, wts, ra, group=4):
    even = node_tables([0, 0, 2, 2, 4, 4, 6, 6])
    odd = node_tables([1, 1, 3, 3, 5, 5, 7, 7])
    plain = node_tables(list(range(8)))
    y_sub = iota((8, 128), 0) % 2
    total = None
    for g in range(n_tiles // group):
        for t in range(g * group, g * group + group):
            cols = slice(128 * t, 128 * t + 128)
            sx, sy, sz = coords_at(t)
            y_of = (host_at(t) // 2) % 2
            keep = y_of == y_sub
            base[0:8, cols] = jnp.where(keep, lagrange(sx, even), 0.0)
            base[8:16, cols] = jnp.where(keep, lagrange(sx, odd), 0.0)
            lb, lc = lagrange(sy, plain), lagrange(sz, plain)
            w = jnp.concatenate([jnp.broadcast_to(lb[b : b + 1], (8, 128)) * lc for b in range(8)], axis=0)
            hi, lo = split(w)
            wts[0:64, cols] = hi
            wts[64:128, cols] = hi
            wts[128:192, cols] = lo
            wts[192:256, cols] = lo
        span = slice(128 * g * group, 128 * (g + 1) * group)
        h = jnp.dot(field, wts[:, span], preferred_element_type=F32)
        for t in range(g * group, g * group + group):
            cols = slice(128 * t, 128 * t + 128)
            sub = slice(128 * (t - g * group), 128 * (t - g * group) + 128)
            code = host_at(t)
            q = (code // 4) * 2 + code % 2
            drag = drag_at(t) * (-MASS)
            at = [q == i for i in range(4)]
            lines = [base[0:8, cols], base[8:16, cols]]
            carried = []
            for c in range(3):
                acc = None
                for a1 in range(2):
                    r = (a1 * 12 + c * 4) * 8
                    v = h[r : r + 8, sub]
                    for i in range(1, 4):
                        v = jnp.where(at[i], h[r + 8 * i : r + 8 * i + 8, sub], v)
                    v = v * lines[a1]
                    acc = v if acc is None else acc + v
                carried.append(jnp.sum(acc, axis=0, keepdims=True))
            emit(t, carried)
            speed = velocity_at(t)
            for c in range(3):
                r = drag * (carried[c] - speed[c])
                for a1 in range(2):
                    v = r * lines[a1]
                    hi = v.astype(BF16).astype(F32)
                    lo = v - hi
                    for part, value in enumerate((hi, lo)):
                        first = ((part * 2 + a1) * 3 + c) * 32
                        rows = jnp.concatenate([jnp.where(at[i], value, 0.0) for i in range(4)], axis=0)
                        ra[first : first + 32, cols] = rows.astype(BF16)
        d = lax.dot_general(
            ra[:, span], wts[64:192, span], (((1,), (1,)), ((), ())), preferred_element_type=F32
        )
        total = d if total is None else total + d
    d = total[0:192] + total[192:384]
    d = d + pltpu.roll(d, 64, 1)
    return jnp.where(iota((96, 128), 1) < 64, d[0:96], d[96:192])


def lists_onehot(mig, store):
    high = []
    lane_row = iota((128, 128), 0)
    for t in range(16):
        idx = mig[t : t + 1, :]
        store[:, 128 * t : 128 * t + 128] = jnp.where(lane_row == (idx & 127), 1.0, 0.0).astype(BF16)
        high.append(idx >> 7)
    return high


def send_kernel(
    fl, co, ve, dr, ho, mi, ta, la, o0, o1, o2, o3, vf, vc, vv, vd, vh, vm, vt, vl, onehot, table, sems
):
    pairs = ((mi, vm), (co, vc), (ve, vv), (dr, vd), (ho, vh), (fl, vf), (ta, vt), (la, vl))
    copies = [pltpu.make_async_copy(src, dst, sems.at[n]) for n, (src, dst) in enumerate(pairs)]
    for copy in copies:
        copy.start()
    copies[0].wait()
    high = lists_onehot(vm, onehot)
    for copy in copies[1:]:
        copy.wait()
    for c in range(3):
        table[pl.ds(c, 16, stride=8), :] = vc[16 * c : 16 * c + 16, :]
        table[pl.ds(3 + c, 16, stride=8), :] = vv[16 * c : 16 * c + 16, :]
    table[pl.ds(6, 16, stride=8), :] = vd[...]
    table[pl.ds(7, 16, stride=8), :] = vh[...].astype(F32)
    hi, lo = split(table[...])
    hi_lo = jnp.concatenate([hi, lo], axis=1)
    odd_d, odd_c = parity("drift"), parity("cross")
    x_lo, x_hi, y_lo, y_hi = pack_faces(functools.partial(tile_of, vf))
    o0[32:48, :] = jnp.where(odd_d, x_hi, x_lo)
    o1[32:48, :] = jnp.where(odd_d, x_lo, x_hi)
    o2[32:48, :] = jnp.where(odd_c, y_hi, y_lo)
    o3[32:48, :] = jnp.where(odd_c, y_lo, y_hi)
    for t in range(4):
        span = onehot[:, 512 * t : 512 * t + 512]
        y = jnp.dot(hi_lo, jnp.concatenate([span, span], axis=0), preferred_element_type=F32)
        found = []
        for d in range(4):
            h = high[4 * t + d]
            g = jnp.zeros((8, 128), F32)
            for row in range(16):
                g = jnp.where(h == row, y[8 * row : 8 * row + 8, 128 * d : 128 * d + 128], g)
            found.append(g)
        rows = slice(8 * t, 8 * t + 8)
        o0[rows, :] = jnp.where(odd_d, found[1], found[0])
        o1[rows, :] = jnp.where(odd_d, found[0], found[1])
        o2[rows, :] = jnp.where(odd_c, found[3], found[2])
        o3[rows, :] = jnp.where(odd_c, found[2], found[3])


def own_kernel(
    fl, co, ve, dr, ho, mi, tab, lane_op, onehot, dep_out, vel_out, base_out, operand_out, car, base, wts, ra
):
    high = [mi[t : t + 1, :] >> 7 for t in range(16)]
    sub16 = iota((16, 128), 0)
    rows = jnp.concatenate([jnp.where(h == sub16, 1.0, 0.0) for h in high], axis=1).astype(BF16)
    listed = lax.dot_general(rows, onehot[...], (((1,), (1,)), ((), ())), preferred_element_type=F32)
    own = jnp.where(listed > 0.5, 0.0, 1.0)
    get = functools.partial(tile_of, fl)
    field = field_operand(get)
    operand_out[...] = field
    drag_own = dr[...] * own

    def emit(t, carried):
        for c in range(3):
            car[16 * c + t : 16 * c + t + 1, :] = carried[c]

    dep_out[...] = couple(
        16,
        lambda t: [row_of(co, 16 * c + t) for c in range(3)],
        lambda t: [row_of(ve, 16 * c + t) for c in range(3)],
        lambda t: jnp.broadcast_to(drag_own[t : t + 1], (8, 128)),
        lambda t: row_of(ho, t),
        field, emit, base, wts, ra,
    )
    for c in range(3):
        r = slice(16 * c, 16 * c + 16)
        vel_out[r, :] = ve[r, :] + dr[...] * (car[r, :] * own - ve[r, :])
    out = local_step(get, tab, lane_op)
    for n, i in enumerate(CXZ):
        base_out[8 * n : 8 * n + 8, :] = out[i]


def host_kernel(r0, r1, r2, r3, operand, dep_in, base_in, u_out, dep_out, o0, o1, o2, o3, base, wts, ra):
    received, sent = (r0, r1, r2, r3), (o0, o1, o2, o3)
    odd_d, odd_c = parity("drift"), parity("cross")
    pick = lambda t, v: row_of(received[t // 4], 8 * (t % 4) + v)

    def emit(t, carried):
        for c in range(3):
            sent[t // 4][4 * (t % 4) + c : 4 * (t % 4) + c + 1, :] = carried[c]
        sent[t // 4][4 * (t % 4) + 3 : 4 * (t % 4) + 4, :] = carried[0]

    dep = dep_in[...] + couple(
        16,
        lambda t: [pick(t, c) for c in range(3)],
        lambda t: [pick(t, 3 + c) for c in range(3)],
        lambda t: pick(t, 6),
        lambda t: pick(t, 7).astype(jnp.int32),
        operand[...], emit, base, wts, ra,
    )
    dep_out[...] = dep
    faces = received_faces(odd_d, odd_c, *[r[32:48, :] for r in received])
    new = {}
    for n, i in enumerate(CXZ):
        r = slice(8 * n, 8 * n + 8)
        new[i] = base_in[r, :] + faces(*i) + 0.5 * dep[r]
        u_out[r, :] = new[i]
    x_lo, x_hi, y_lo, y_hi = pack_faces(lambda c, x, z: new[c, x, z])
    o0[16:32, :] = jnp.where(odd_d, x_hi, x_lo)
    o1[16:32, :] = jnp.where(odd_d, x_lo, x_hi)
    o2[16:32, :] = jnp.where(odd_c, y_hi, y_lo)
    o3[16:32, :] = jnp.where(odd_c, y_lo, y_hi)


def second_kernel(u, dep, tab, lane_op, out_ref):
    out = local_step(functools.partial(tile_of, u), tab, lane_op)
    for n, i in enumerate(CXZ):
        r = slice(8 * n, 8 * n + 8)
        out_ref[r, :] = out[i] + 0.5 * dep[r, :]


def last_kernel(r0, r1, r2, r3, base, vel, dr, mi, onehot, fluid_out, vel_out):
    odd_d, odd_c = parity("drift"), parity("cross")
    faces = received_faces(odd_d, odd_c, *[r[16:32, :] for r in (r0, r1, r2, r3)])
    for n, i in enumerate(CXZ):
        r = slice(8 * n, 8 * n + 8)
        fluid_out[r, :] = base[r, :] + faces(*i)
    sub16 = iota((16, 128), 0)
    columns = []
    for t in range(4):
        rows = slice(4 * t, 4 * t + 4)
        back = [
            jnp.where(odd_d, r1[rows, :], r0[rows, :]),
            jnp.where(odd_d, r0[rows, :], r1[rows, :]),
            jnp.where(odd_c, r3[rows, :], r2[rows, :]),
            jnp.where(odd_c, r2[rows, :], r3[rows, :]),
        ]
        for d in range(4):
            at = (mi[4 * t + d : 4 * t + d + 1, :] >> 7) == sub16
            columns.append(jnp.concatenate([jnp.where(at, back[d][c : c + 1], 0.0) for c in range(3)], axis=0))
    hi, lo = split(jnp.concatenate(columns, axis=1))
    put = lax.dot_general(
        jnp.concatenate([hi, lo], axis=0), onehot[...], (((1,), (1,)), ((), ())), preferred_element_type=F32
    )
    put = put[0:48] + put[48:96]
    for c in range(3):
        r = slice(16 * c, 16 * c + 16)
        vel_out[r, :] = vel[r, :] + dr[...] * put[r]


def shape(rows, dtype=F32, lanes=128):
    return jax.ShapeDtypeStruct((rows, lanes), dtype)


def call(kernel, outs, scratch=(), in_specs=None, cost=0, **kw):
    if in_specs is not None:
        kw["in_specs"] = in_specs
    return pl.pallas_call(
        kernel,
        out_shape=outs,
        scratch_shapes=list(scratch),
        cost_estimate=pl.CostEstimate(flops=cost, bytes_accessed=0, transcendentals=0),
        compiler_params=pltpu.CompilerParams(vmem_limit_bytes=VMEM),
        **kw,
    )


def swap(block, axis, odd):
    count = lax.axis_size(axis)
    pairs = []
    for i in range(odd, count + odd, 2):
        first, other = i % count, (i + 1) % count
        pairs += [(first, other), (other, first)]
    return lax.ppermute(block, axis, pairs)


def exchange(blocks):
    order = (("drift", 1), ("drift", 0), ("cross", 1), ("cross", 0))
    return [swap(block, axis, odd) for block, (axis, odd) in zip(blocks, order)]


def per_device(fluid_field, coords, velocity, drag_factor, host_ids, migrants):
    field = fluid_field.reshape(3, 2, 2, 8, 128).transpose(0, 1, 3, 2, 4).reshape(96, 128)
    args = (
        field,
        coords.reshape(48, 128),
        velocity.reshape(48, 128),
        drag_factor.reshape(16, 128),
        host_ids.reshape(16, 128),
        migrants.reshape(4, 4, 128).transpose(1, 0, 2).reshape(16, 128),
    )
    couple_scratch = [pltpu.VMEM((16, 2048), F32), pltpu.VMEM((256, 2048), BF16), pltpu.VMEM((384, 2048), BF16)]
    args += tuple(jnp.asarray(t) for t in operator_tables())
    outs = call(
        send_kernel,
        [shape(48)] * 4 + [shape(*a.shape[:1], a.dtype, a.shape[1]) for a in args] + [shape(128, BF16, 2048)],
        [pltpu.VMEM((128, 128), F32), pltpu.SemaphoreType.DMA((8,))],
        in_specs=[pl.BlockSpec(memory_space=pl.ANY)] * 8,
    )(*(pltpu.with_memory_space_constraint(a, pltpu.HBM) for a in args))
    sends, args, onehot = outs[:4], outs[4:12], outs[12]
    tab, lane_op = args[6:]
    received = exchange(sends)
    dep, vel, base, operand = call(
        own_kernel,
        [shape(96), shape(48), shape(96), shape(192, BF16, 256)],
        [pltpu.VMEM((48, 128), F32)] + couple_scratch,
        cost=1 << 31,
    )(*args, onehot)
    u, dep, *sends = call(host_kernel, [shape(96)] * 2 + [shape(32)] * 4, couple_scratch)(
        *received, operand, dep, base
    )
    received = exchange(sends)
    base = call(second_kernel, shape(96), cost=1 << 30)(u, dep, tab, lane_op)
    fluid, vel = call(last_kernel, [shape(96), shape(48)])(*received, base, vel, args[3], args[5], onehot)
    fluid = fluid.reshape(3, 2, 8, 2, 128).transpose(0, 1, 3, 2, 4).reshape(3, 2, 2, 1024)
    return fluid, vel.reshape(3, 1, 1, 2048)


def solution(mesh):
    field = P(None, "drift", "cross", None)
    scalar = P("drift", "cross", None)
    return jax.shard_map(
        per_device,
        mesh=mesh,
        in_specs=(field, field, field, scalar, scalar, P("drift", "cross", None, None)),
        out_specs=(field, field),
        check_vma=False,
    )
```

```python
import functools

import jax
import jax.numpy as jnp
import numpy as np
from jax import lax
from jax.experimental import pallas as pl
from jax.experimental.pallas import tpu as pltpu
from jax.sharding import PartitionSpec as P


F32 = jnp.float32
BF16 = jnp.bfloat16
MASS = 4.0
DIFF = 0.002
PEN = 0.05
VMEM = 24 << 20

NODES = -np.cos(np.pi * np.arange(8) / 7.0)
DENOM = np.array([np.prod([NODES[t] - NODES[m] for m in range(8) if m != t]) for t in range(8)])


def second_np():
    end = np.where((np.arange(8) == 0) | (np.arange(8) == 7), 2.0, 1.0)
    d = np.zeros((8, 8))
    for i in range(8):
        for m in range(8):
            if i != m:
                d[i, m] = end[i] / end[m] * (-1.0) ** (i + m) / (NODES[i] - NODES[m])
    d -= np.diag(d.sum(axis=1))
    return d @ d


def operator_tables():
    s = second_np()
    tab = np.zeros((2, 4, 8, 128))
    a1 = np.arange(128) // 64
    b = np.arange(128) // 8 % 8
    k = np.arange(128) % 8
    for sub in range(8):
        a2 = sub // 2
        a = 2 * a2 + a1
        for step in range(4):
            other = (a2 - step) % 4
            tab[0, step, sub] = DIFF * s[a, 2 * other + a1]
            tab[1, step, sub] = DIFF * s[a, 2 * other + 1 - a1]
        mult = ((a == 0) | (a == 7)) * 1.0 + ((b == 0) | (b == 7)) + ((k == 0) | (k == 7))
        tab[0, 0, sub] += 1.0 - PEN * mult
    eye = np.eye(8)
    side = DIFF * (np.kron(s, eye) + np.kron(eye, s))
    lane = np.kron(np.eye(2), side).T.astype(np.float32)
    hi = lane.astype(jnp.bfloat16)
    lo = (lane - hi.astype(np.float32)).astype(jnp.bfloat16)
    half = np.concatenate([hi, lo], axis=1)
    return tab.reshape(64, 128).astype(np.float32), np.concatenate([half, half], axis=0)


def iota(shape, dim):
    return lax.broadcasted_iota(jnp.int32, shape, dim)


def split(x):
    hi = x.astype(BF16)
    lo = (x - hi.astype(F32)).astype(BF16)
    return hi, lo


def row_of(ref, r):
    return jnp.broadcast_to(ref[r : r + 1, :], (8, 128))


def sublane_table(values):
    sub = iota((8, 128), 0)
    out = jnp.full((8, 128), float(values[0]), F32)
    for i in range(1, 8):
        out = jnp.where(sub == i, float(values[i]), out)
    return out


def node_tables(order):
    partners = [[m for m in range(8) if m != t] for t in order]
    tables = [sublane_table([NODES[p[j]] for p in partners]) for j in range(7)]
    return tables, sublane_table([1.0 / DENOM[t] for t in order])


def lagrange(s, tables):
    nodes, scale = tables
    out = (s - nodes[0]) * scale
    for t in nodes[1:]:
        out = out * (s - t)
    return out


def tile_of(ref, c, x, z):
    r = ((c * 2 + x) * 2 + z) * 8
    return ref[r : r + 8, :]


CXZ = [(c, x, z) for c in range(3) for x in range(2) for z in range(2)]


def parity(axis):
    return lax.rem(lax.axis_index(axis), 2) == 1


def face_masks():
    sub, lane = iota((8, 128), 0), iota((8, 128), 1)
    a2, y, a1, b, k = sub // 2, sub % 2, lane // 64, lane // 8 % 8, lane % 8
    pick = lambda cond: jnp.where(cond, PEN, 0.0).astype(F32)
    return dict(
        x_lo=pick((a2 == 0) & (a1 == 0)),
        x_hi=pick((a2 == 3) & (a1 == 1)),
        y_lo=pick((y == 0) & (b == 0)),
        y_hi=pick((y == 1) & (b == 7)),
        y_in_hi=pick((y == 0) & (b == 7)),
        y_in_lo=pick((y == 1) & (b == 0)),
        z_lo=pick(k == 0),
        z_hi=pick(k == 7),
    )


def pack_faces(get):
    lane = iota((8, 128), 1)
    b = lane // 8 % 8
    low = [get(c, 0, z)[0:2] for c in range(3) for z in range(2)]
    high = [get(c, 1, z)[6:8] for c in range(3) for z in range(2)]
    fill = jnp.zeros((4, 128), F32)
    x_lo = pltpu.roll(jnp.concatenate(low + [fill], axis=0), 64, 1)
    x_hi = pltpu.roll(jnp.concatenate(high + [fill], axis=0), 64, 1)
    y_lo, y_hi = [], []
    for group in range(2):
        lo = hi = None
        for i in range(6):
            v = get(*CXZ[group * 6 + i])
            here = b == i
            to_lo = v if i == 0 else pltpu.roll(v, 8 * i, 1)
            to_hi = pltpu.roll(v, (8 * i + 72) % 128, 1)
            lo = to_lo if lo is None else jnp.where(here, to_lo, lo)
            hi = to_hi if hi is None else jnp.where(here, to_hi, hi)
        y_lo.append(pltpu.roll(lo, 1, 0))
        y_hi.append(pltpu.roll(hi, 7, 0))
    return x_lo, x_hi, jnp.concatenate(y_lo, axis=0), jnp.concatenate(y_hi, axis=0)


def face_part(along, up, message):
    m = face_masks()
    if along == "drift":
        sides = (jnp.where(up, 0.0, m["x_lo"]), jnp.where(up, m["x_hi"], 0.0))

        def at(c, x, z):
            r = 2 * (c * 2 + z)
            return jnp.concatenate([message[r : r + 2]] * 4, axis=0) * sides[x]

        return at
    side = jnp.where(up, m["y_hi"], m["y_lo"])
    pieces = [message[8 * g : 8 * g + 8] for g in range(2)]
    pieces = [jnp.where(up, pltpu.roll(v, 56, 1), v) for v in pieces]

    def at(c, x, z):
        index = (c * 2 + x) * 2 + z
        g, i = index // 6, index % 6
        return (pltpu.roll(pieces[g], 128 - 8 * i, 1) if i else pieces[g]) * side

    return at


def local_step(get, tab, lane_op):
    m = face_masks()
    whole = jnp.concatenate([get(*i) for i in CXZ], axis=0)
    hi, lo = split(whole)
    product = jnp.dot(jnp.concatenate([hi, lo], axis=1), lane_op[...], preferred_element_type=F32)
    product = product[:, 0:128] + product[:, 128:256]
    turned = {}
    for i in CXZ:
        v = get(*i)
        w = pltpu.roll(v, 64, 1)
        turned[i] = (
            [v] + [pltpu.roll(v, 2 * s, 0) for s in range(1, 4)],
            [w] + [pltpu.roll(w, 2 * s, 0) for s in range(1, 4)],
        )
    out = {}
    for n, (c, x, z) in enumerate(CXZ):
        v = turned[c, x, z][0][0]
        total = product[8 * n : 8 * n + 8]
        for kind in range(2):
            for s in range(4):
                r = (kind * 4 + s) * 8
                total = total + turned[c, x, z][kind][s] * tab[r : r + 8, :]
        beside = turned[c, 1 - x, z][1]
        total = total + (beside[3] * m["x_hi"] if x == 0 else beside[1] * m["x_lo"])
        total = total + pltpu.roll(pltpu.roll(v, 56, 1), 7, 0) * m["y_in_hi"]
        total = total + pltpu.roll(pltpu.roll(v, 72, 1), 1, 0) * m["y_in_lo"]
        across = turned[c, x, 1 - z][0][0]
        if z == 0:
            total = total + pltpu.roll(across, 7, 1) * m["z_hi"]
        else:
            total = total + pltpu.roll(across, 121, 1) * m["z_lo"]
        out[c, x, z] = total
    return out


def field_operand(get):
    lane = iota((96, 128), 1)
    whole = jnp.concatenate([get(*i) for i in CXZ], axis=0)
    hi = whole.astype(BF16).astype(F32)
    lo = whole - hi
    first = jnp.where(lane < 64, hi, pltpu.roll(lo, 64, 1)).astype(BF16)
    second = jnp.where(lane < 64, pltpu.roll(hi, 64, 1), lo).astype(BF16)
    rows = jnp.concatenate([first, second], axis=0)
    return jnp.concatenate([rows, rows], axis=1)


def couple(n_tiles, coords_at, velocity_at, drag_at, host_at, field, emit, base, wts, ra, group=8):
    even = node_tables([0, 0, 2, 2, 4, 4, 6, 6])
    odd = node_tables([1, 1, 3, 3, 5, 5, 7, 7])
    plain = node_tables(list(range(8)))
    y_sub = iota((8, 128), 0) % 2
    total = None
    for g in range(n_tiles // group):
        for t in range(g * group, g * group + group):
            cols = slice(128 * t, 128 * t + 128)
            sx, sy, sz = coords_at(t)
            y_of = (host_at(t) // 2) % 2
            keep = y_of == y_sub
            base[0:8, cols] = jnp.where(keep, lagrange(sx, even), 0.0)
            base[8:16, cols] = jnp.where(keep, lagrange(sx, odd), 0.0)
            lb, lc = lagrange(sy, plain), lagrange(sz, plain)
            w = jnp.concatenate([jnp.broadcast_to(lb[b : b + 1], (8, 128)) * lc for b in range(8)], axis=0)
            hi, lo = split(w)
            wts[0:64, cols] = hi
            wts[64:128, cols] = hi
            wts[128:192, cols] = lo
            wts[192:256, cols] = lo
        span = slice(128 * g * group, 128 * (g + 1) * group)
        h = jnp.dot(field, wts[:, span], preferred_element_type=F32)
        for t in range(g * group, g * group + group):
            cols = slice(128 * t, 128 * t + 128)
            sub = slice(128 * (t - g * group), 128 * (t - g * group) + 128)
            code = host_at(t)
            q = (code // 4) * 2 + code % 2
            drag = drag_at(t) * (-MASS)
            at = [q == i for i in range(4)]
            lines = [base[0:8, cols], base[8:16, cols]]
            carried = []
            for c in range(3):
                acc = None
                for a1 in range(2):
                    r = (a1 * 12 + c * 4) * 8
                    v = h[r : r + 8, sub]
                    for i in range(1, 4):
                        v = jnp.where(at[i], h[r + 8 * i : r + 8 * i + 8, sub], v)
                    v = v * lines[a1]
                    acc = v if acc is None else acc + v
                carried.append(jnp.sum(acc, axis=0, keepdims=True))
            emit(t, carried)
            speed = velocity_at(t)
            for c in range(3):
                r = drag * (carried[c] - speed[c])
                for a1 in range(2):
                    v = r * lines[a1]
                    hi = v.astype(BF16).astype(F32)
                    lo = v - hi
                    for part, value in enumerate((hi, lo)):
                        first = ((part * 2 + a1) * 3 + c) * 32
                        rows = jnp.concatenate([jnp.where(at[i], value, 0.0) for i in range(4)], axis=0)
                        ra[first : first + 32, cols] = rows.astype(BF16)
        d = lax.dot_general(
            ra[:, span], wts[64:192, span], (((1,), (1,)), ((), ())), preferred_element_type=F32
        )
        total = d if total is None else total + d
    d = total[0:192] + total[192:384]
    d = d + pltpu.roll(d, 64, 1)
    return jnp.where(iota((96, 128), 1) < 64, d[0:96], d[96:192])


ALONG = ("drift", "drift", "cross", "cross")
FACES = 32
BACK = 16


def ups():
    odd_d, odd_c = parity("drift"), parity("cross")
    return odd_d, jnp.logical_not(odd_d), odd_c, jnp.logical_not(odd_c)


def towards(s, up):
    return 2 * (s // 2) + up.astype(jnp.int32)


def faces_to(s, up, packed):
    low, high = packed[2 * (s // 2) : 2 * (s // 2) + 2]
    return jnp.where(up, high, low)


def gather(s, hi_lo, lists, onehot, out):
    lane_row = iota((128, 128), 0)
    high = []
    for t in range(4):
        idx = lists[4 * s + t : 4 * s + t + 1, :]
        cols = slice(512 * s + 128 * t, 512 * s + 128 * t + 128)
        onehot[:, cols] = jnp.where(lane_row == (idx & 127), 1.0, 0.0).astype(BF16)
        high.append(idx >> 7)
    span = onehot[:, 512 * s : 512 * s + 512]
    y = jnp.dot(hi_lo, jnp.concatenate([span, span], axis=0), preferred_element_type=F32)
    for t in range(4):
        g = jnp.zeros((8, 128), F32)
        for row in range(16):
            g = jnp.where(high[t] == row, y[8 * row : 8 * row + 8, 128 * t : 128 * t + 128], g)
        out[8 * t : 8 * t + 8, :] = g


def send_kernel(
    fl, co, ve, dr, ho, mi, ta, la, o0, o1, o2, o3, vf, vc, vv, vd, vh, lists, vt, vl, onehot, vm, table, sems
):
    pairs = ((mi, vm), (co, vc), (ve, vv), (dr, vd), (ho, vh), (fl, vf), (ta, vt), (la, vl))
    copies = [pltpu.make_async_copy(src, dst, sems.at[n]) for n, (src, dst) in enumerate(pairs)]
    for copy in copies:
        copy.start()
    up = ups()
    copies[0].wait()
    for s in range(4):
        for t in range(4):
            lists[4 * s + t : 4 * s + t + 1, :] = vm[pl.ds(4 * t + towards(s, up[s]), 1), :]
    for copy in copies[1:]:
        copy.wait()
    for c in range(3):
        table[pl.ds(c, 16, stride=8), :] = vc[16 * c : 16 * c + 16, :]
        table[pl.ds(3 + c, 16, stride=8), :] = vv[16 * c : 16 * c + 16, :]
    table[pl.ds(6, 16, stride=8), :] = vd[...]
    table[pl.ds(7, 16, stride=8), :] = vh[...].astype(F32)
    parts = jnp.concatenate(split(table[...]), axis=1)
    packed = pack_faces(functools.partial(tile_of, vf))
    for s, out in enumerate((o0, o1, o2, o3)):
        out[FACES:, :] = faces_to(s, up[s], packed)
        gather(s, parts, lists, onehot, out)


def own_kernel(
    fl, co, ve, dr, ho, lists, tab, lane_op, onehot, dep_out, vel_out, base_out, operand_out, car, base, wts, ra
):
    sub16 = iota((16, 128), 0)
    rows = [jnp.where((lists[t : t + 1, :] >> 7) == sub16, 1.0, 0.0) for t in range(16)]
    rows = jnp.concatenate(rows, axis=1).astype(BF16)
    listed = lax.dot_general(rows, onehot[...], (((1,), (1,)), ((), ())), preferred_element_type=F32)
    own = jnp.where(listed > 0.5, 0.0, 1.0)
    get = functools.partial(tile_of, fl)
    field = field_operand(get)
    operand_out[...] = field
    drag_own = dr[...] * own

    def emit(t, carried):
        for c in range(3):
            car[16 * c + t : 16 * c + t + 1, :] = carried[c]

    dep_out[...] = couple(
        16,
        lambda t: [row_of(co, 16 * c + t) for c in range(3)],
        lambda t: [row_of(ve, 16 * c + t) for c in range(3)],
        lambda t: jnp.broadcast_to(drag_own[t : t + 1], (8, 128)),
        lambda t: row_of(ho, t),
        field, emit, base, wts, ra,
    )
    for c in range(3):
        r = slice(16 * c, 16 * c + 16)
        vel_out[r, :] = ve[r, :] + dr[...] * (car[r, :] * own - ve[r, :])
    out = local_step(get, tab, lane_op)
    for n, i in enumerate(CXZ):
        base_out[8 * n : 8 * n + 8, :] = out[i]


def host_lists(received, back, dep_in, operand, scratch):
    pick = lambda t, v: row_of(received[t // 4], 8 * (t % 4) + v)

    def emit(t, carried):
        rows = carried + [carried[0]]
        for c in range(4):
            back[t // 4][4 * (t % 4) + c : 4 * (t % 4) + c + 1, :] = rows[c]

    return dep_in[...] + couple(
        4 * len(received),
        lambda t: [pick(t, c) for c in range(3)],
        lambda t: [pick(t, 3 + c) for c in range(3)],
        lambda t: pick(t, 6),
        lambda t: pick(t, 7).astype(jnp.int32),
        operand[...], emit, *scratch,
    )


def near_kernel(r1, r3, operand, dep_in, dep_out, b1, b3, *scratch):
    dep_out[...] = host_lists((r1, r3), (b1, b3), dep_in, operand, scratch)


def far_kernel(r0, r1, r2, r3, operand, dep_in, base_in, b1, b3, u_out, dep_out, o0, o1, o2, o3, *scratch):
    dep = host_lists((r0, r2), (o0, o2), dep_in, operand, scratch)
    dep_out[...] = dep
    up = ups()
    parts = [face_part(ALONG[s], up[s], r[FACES:, :]) for s, r in enumerate((r0, r1, r2, r3))]
    new = {}
    for n, i in enumerate(CXZ):
        r = slice(8 * n, 8 * n + 8)
        new[i] = base_in[r, :] + sum(part(*i) for part in parts) + 0.5 * dep[r]
        u_out[r, :] = new[i]
    packed = pack_faces(lambda c, x, z: new[c, x, z])
    o1[0:BACK, :] = b1[...]
    o3[0:BACK, :] = b3[...]
    for s, out in enumerate((o0, o1, o2, o3)):
        out[BACK:, :] = faces_to(s, up[s], packed)


def second_kernel(u, dep, tab, lane_op, out_ref):
    out = local_step(functools.partial(tile_of, u), tab, lane_op)
    for n, i in enumerate(CXZ):
        r = slice(8 * n, 8 * n + 8)
        out_ref[r, :] = out[i] + 0.5 * dep[r, :]


def last_kernel(r0, r1, r2, r3, base, vel, dr, lists, onehot, fluid_out, vel_out):
    received = [r[...] for r in (r0, r1, r2, r3)]
    up = ups()
    parts = [face_part(ALONG[s], up[s], received[s][BACK:]) for s in range(4)]
    for n, i in enumerate(CXZ):
        fluid_out[8 * n : 8 * n + 8, :] = tile_of(base, *i) + sum(part(*i) for part in parts)
    sub16 = iota((16, 128), 0)
    columns = []
    for s in range(4):
        for t in range(4):
            at = (lists[4 * s + t : 4 * s + t + 1, :] >> 7) == sub16
            back = received[s][4 * t : 4 * t + 4]
            columns.append(jnp.concatenate([jnp.where(at, back[c : c + 1], 0.0) for c in range(3)], axis=0))
    rows = jnp.concatenate(split(jnp.concatenate(columns, axis=1)), axis=0)
    put = lax.dot_general(rows, onehot[...], (((1,), (1,)), ((), ())), preferred_element_type=F32)
    put = put[0:48] + put[48:96]
    for c in range(3):
        r = slice(16 * c, 16 * c + 16)
        vel_out[r, :] = vel[r, :] + dr[...] * put[r]


def shape(rows, dtype=F32, lanes=128):
    return jax.ShapeDtypeStruct((rows, lanes), dtype)


def call(kernel, outs, scratch=(), in_specs=None, cost=0, **kw):
    if in_specs is not None:
        kw["in_specs"] = in_specs
    return pl.pallas_call(
        kernel,
        out_shape=outs,
        scratch_shapes=list(scratch),
        cost_estimate=pl.CostEstimate(flops=cost, bytes_accessed=0, transcendentals=0),
        compiler_params=pltpu.CompilerParams(vmem_limit_bytes=VMEM),
        **kw,
    )


def exchange(messages):
    rows, columns = lax.axis_size("drift"), lax.axis_size("cross")

    def partner(i, j, s):
        if s < 2:
            return (i + (1 if i % 2 != s else -1)) % rows, j
        return i, (j + (1 if j % 2 != s - 2 else -1)) % columns

    received = []
    for n, message in enumerate(messages):
        pairs = []
        for i in range(rows):
            for j in range(columns):
                k, l = partner(i, j, n)
                pairs.append((i * columns + j, k * columns + l))
        received.append(lax.ppermute(message, ("drift", "cross"), pairs))
    return received


def per_device(fluid_field, coords, velocity, drag_factor, host_ids, migrants):
    field = fluid_field.reshape(3, 2, 2, 8, 128).transpose(0, 1, 3, 2, 4).reshape(96, 128)
    args = (
        field,
        coords.reshape(48, 128),
        velocity.reshape(48, 128),
        drag_factor.reshape(16, 128),
        host_ids.reshape(16, 128),
        migrants.reshape(4, 4, 128).transpose(1, 0, 2).reshape(16, 128),
    )
    args += tuple(jnp.asarray(t) for t in operator_tables())
    back = shape(BACK)

    def scratch(tiles):
        n = 128 * tiles
        return [pltpu.VMEM((16, n), F32), pltpu.VMEM((256, n), BF16), pltpu.VMEM((384, n), BF16)]

    outs = call(
        send_kernel,
        [shape(48)] * 4
        + [shape(a.shape[0], a.dtype, a.shape[1]) for a in args]
        + [shape(128, BF16, 2048)],
        [
            pltpu.VMEM((16, 128), jnp.int32),
            pltpu.VMEM((128, 128), F32),
            pltpu.SemaphoreType.DMA((8,)),
        ],
        in_specs=[pl.BlockSpec(memory_space=pl.ANY)] * 8,
    )(*(pltpu.with_memory_space_constraint(a, pltpu.HBM) for a in args))
    sends, args, onehot = outs[:4], outs[4:12], outs[12]
    drag, lists, tab, lane_op = args[3], *args[5:]
    r0, r1, r2, r3 = exchange(sends)
    dep, vel, base, operand = call(
        own_kernel,
        [shape(96), shape(48), shape(96), shape(192, BF16, 256)],
        [pltpu.VMEM((48, 128), F32)] + scratch(16),
        cost=1 << 31,
    )(*args, onehot)
    dep, *rest = call(near_kernel, [shape(96)] + [back] * 2, scratch(8), cost=1 << 30)(r1, r3, operand, dep)
    u, dep, *sends = call(far_kernel, [shape(96)] * 2 + [shape(32)] * 4, scratch(8))(
        r0, r1, r2, r3, operand, dep, base, *rest
    )
    received = exchange(sends)
    base = call(second_kernel, shape(96), cost=1 << 30)(u, dep, tab, lane_op)
    fluid, vel = call(last_kernel, [shape(96), shape(48)])(*received, base, vel, drag, lists, onehot)
    fluid = fluid.reshape(3, 2, 8, 2, 128).transpose(0, 1, 3, 2, 4).reshape(3, 2, 2, 1024)
    return fluid, vel.reshape(3, 1, 1, 2048)


def solution(mesh):
    field = P(None, "drift", "cross", None)
    scalar = P("drift", "cross", None)
    return jax.shard_map(
        per_device,
        mesh=mesh,
        in_specs=(field, field, field, scalar, scalar, P("drift", "cross", None, None)),
        out_specs=(field, field),
        check_vma=False,
    )
```

```python
import functools

import jax
import jax.numpy as jnp
import numpy as np
from jax import lax
from jax.experimental import pallas as pl
from jax.experimental.pallas import tpu as pltpu
from jax.sharding import PartitionSpec as P


F32 = jnp.float32
BF16 = jnp.bfloat16
MASS = 4.0
DIFF = 0.002
PEN = 0.05
VMEM = 24 << 20

NODES = -np.cos(np.pi * np.arange(8) / 7.0)
DENOM = np.array([np.prod([NODES[t] - NODES[m] for m in range(8) if m != t]) for t in range(8)])


def second_np():
    end = np.where((np.arange(8) == 0) | (np.arange(8) == 7), 2.0, 1.0)
    d = np.zeros((8, 8))
    for i in range(8):
        for m in range(8):
            if i != m:
                d[i, m] = end[i] / end[m] * (-1.0) ** (i + m) / (NODES[i] - NODES[m])
    d -= np.diag(d.sum(axis=1))
    return d @ d


def operator_tables():
    s = second_np()
    tab = np.zeros((2, 4, 8, 128))
    a1 = np.arange(128) // 64
    b = np.arange(128) // 8 % 8
    k = np.arange(128) % 8
    for sub in range(8):
        a2 = sub // 2
        a = 2 * a2 + a1
        for step in range(4):
            other = (a2 - step) % 4
            tab[0, step, sub] = DIFF * s[a, 2 * other + a1]
            tab[1, step, sub] = DIFF * s[a, 2 * other + 1 - a1]
        mult = ((a == 0) | (a == 7)) * 1.0 + ((b == 0) | (b == 7)) + ((k == 0) | (k == 7))
        tab[0, 0, sub] += 1.0 - PEN * mult
    eye = np.eye(8)
    side = DIFF * (np.kron(s, eye) + np.kron(eye, s))
    lane = np.kron(np.eye(2), side).T.astype(np.float32)
    hi = lane.astype(jnp.bfloat16)
    lo = (lane - hi.astype(np.float32)).astype(jnp.bfloat16)
    half = np.concatenate([hi, lo], axis=1)
    return tab.reshape(64, 128).astype(np.float32), np.concatenate([half, half], axis=0)


def iota(shape, dim):
    return lax.broadcasted_iota(jnp.int32, shape, dim)


def split(x):
    hi = x.astype(BF16)
    lo = (x - hi.astype(F32)).astype(BF16)
    return hi, lo


def row_of(ref, r):
    return jnp.broadcast_to(ref[r : r + 1, :], (8, 128))


def sublane_table(values):
    sub = iota((8, 128), 0)
    out = jnp.full((8, 128), float(values[0]), F32)
    for i in range(1, 8):
        out = jnp.where(sub == i, float(values[i]), out)
    return out


def node_tables(order):
    partners = [[m for m in range(8) if m != t] for t in order]
    tables = [sublane_table([NODES[p[j]] for p in partners]) for j in range(7)]
    return tables, sublane_table([1.0 / DENOM[t] for t in order])


def lagrange(s, tables):
    nodes, scale = tables
    out = (s - nodes[0]) * scale
    for t in nodes[1:]:
        out = out * (s - t)
    return out


def tile_of(ref, c, x, z):
    r = ((c * 2 + x) * 2 + z) * 8
    return ref[r : r + 8, :]


CXZ = [(c, x, z) for c in range(3) for x in range(2) for z in range(2)]


def parity(axis):
    return lax.rem(lax.axis_index(axis), 2) == 1


def face_masks():
    sub, lane = iota((8, 128), 0), iota((8, 128), 1)
    a2, y, a1, b, k = sub // 2, sub % 2, lane // 64, lane // 8 % 8, lane % 8
    pick = lambda cond: jnp.where(cond, PEN, 0.0).astype(F32)
    return dict(
        x_lo=pick((a2 == 0) & (a1 == 0)),
        x_hi=pick((a2 == 3) & (a1 == 1)),
        y_lo=pick((y == 0) & (b == 0)),
        y_hi=pick((y == 1) & (b == 7)),
        y_in_hi=pick((y == 0) & (b == 7)),
        y_in_lo=pick((y == 1) & (b == 0)),
        z_lo=pick(k == 0),
        z_hi=pick(k == 7),
    )


def pack_faces(get):
    lane = iota((8, 128), 1)
    b = lane // 8 % 8
    low = [get(c, 0, z)[0:2] for c in range(3) for z in range(2)]
    high = [get(c, 1, z)[6:8] for c in range(3) for z in range(2)]
    fill = jnp.zeros((4, 128), F32)
    x_lo = pltpu.roll(jnp.concatenate(low + [fill], axis=0), 64, 1)
    x_hi = pltpu.roll(jnp.concatenate(high + [fill], axis=0), 64, 1)
    y_lo, y_hi = [], []
    for group in range(2):
        lo = hi = None
        for i in range(6):
            v = get(*CXZ[group * 6 + i])
            here = b == i
            to_lo = v if i == 0 else pltpu.roll(v, 8 * i, 1)
            to_hi = pltpu.roll(v, (8 * i + 72) % 128, 1)
            lo = to_lo if lo is None else jnp.where(here, to_lo, lo)
            hi = to_hi if hi is None else jnp.where(here, to_hi, hi)
        y_lo.append(pltpu.roll(lo, 1, 0))
        y_hi.append(pltpu.roll(hi, 7, 0))
    return x_lo, x_hi, jnp.concatenate(y_lo, axis=0), jnp.concatenate(y_hi, axis=0)


def face_part(along, up, message):
    m = face_masks()
    if along == "drift":
        sides = (jnp.where(up, 0.0, m["x_lo"]), jnp.where(up, m["x_hi"], 0.0))

        def at(c, x, z):
            r = 2 * (c * 2 + z)
            return jnp.concatenate([message[r : r + 2]] * 4, axis=0) * sides[x]

        return at
    side = jnp.where(up, m["y_hi"], m["y_lo"])
    pieces = [message[8 * g : 8 * g + 8] for g in range(2)]
    pieces = [jnp.where(up, pltpu.roll(v, 56, 1), v) for v in pieces]

    def at(c, x, z):
        index = (c * 2 + x) * 2 + z
        g, i = index // 6, index % 6
        return (pltpu.roll(pieces[g], 128 - 8 * i, 1) if i else pieces[g]) * side

    return at


def local_step(get, tab, lane_op):
    m = face_masks()
    whole = jnp.concatenate([get(*i) for i in CXZ], axis=0)
    hi, lo = split(whole)
    product = jnp.dot(jnp.concatenate([hi, lo], axis=1), lane_op[...], preferred_element_type=F32)
    product = product[:, 0:128] + product[:, 128:256]
    turned = {}
    for i in CXZ:
        v = get(*i)
        w = pltpu.roll(v, 64, 1)
        turned[i] = (
            [v] + [pltpu.roll(v, 2 * s, 0) for s in range(1, 4)],
            [w] + [pltpu.roll(w, 2 * s, 0) for s in range(1, 4)],
        )
    out = {}
    for n, (c, x, z) in enumerate(CXZ):
        v = turned[c, x, z][0][0]
        total = product[8 * n : 8 * n + 8]
        for kind in range(2):
            for s in range(4):
                r = (kind * 4 + s) * 8
                total = total + turned[c, x, z][kind][s] * tab[r : r + 8, :]
        beside = turned[c, 1 - x, z][1]
        total = total + (beside[3] * m["x_hi"] if x == 0 else beside[1] * m["x_lo"])
        total = total + pltpu.roll(pltpu.roll(v, 56, 1), 7, 0) * m["y_in_hi"]
        total = total + pltpu.roll(pltpu.roll(v, 72, 1), 1, 0) * m["y_in_lo"]
        across = turned[c, x, 1 - z][0][0]
        if z == 0:
            total = total + pltpu.roll(across, 7, 1) * m["z_hi"]
        else:
            total = total + pltpu.roll(across, 121, 1) * m["z_lo"]
        out[c, x, z] = total
    return out


def field_operand(get):
    lane = iota((96, 128), 1)
    whole = jnp.concatenate([get(*i) for i in CXZ], axis=0)
    hi = whole.astype(BF16).astype(F32)
    lo = whole - hi
    first = jnp.where(lane < 64, hi, pltpu.roll(lo, 64, 1)).astype(BF16)
    second = jnp.where(lane < 64, pltpu.roll(hi, 64, 1), lo).astype(BF16)
    rows = jnp.concatenate([first, second], axis=0)
    return jnp.concatenate([rows, rows], axis=1)


def couple(n_tiles, coords_at, velocity_at, drag_at, host_at, field, emit, base, wts, ra, group=8):
    even = node_tables([0, 0, 2, 2, 4, 4, 6, 6])
    odd = node_tables([1, 1, 3, 3, 5, 5, 7, 7])
    plain = node_tables(list(range(8)))
    y_sub = iota((8, 128), 0) % 2
    total = None
    for g in range(n_tiles // group):
        for t in range(g * group, g * group + group):
            cols = slice(128 * t, 128 * t + 128)
            sx, sy, sz = coords_at(t)
            y_of = (host_at(t) // 2) % 2
            keep = y_of == y_sub
            base[0:8, cols] = jnp.where(keep, lagrange(sx, even), 0.0)
            base[8:16, cols] = jnp.where(keep, lagrange(sx, odd), 0.0)
            lb, lc = lagrange(sy, plain), lagrange(sz, plain)
            w = jnp.concatenate([jnp.broadcast_to(lb[b : b + 1], (8, 128)) * lc for b in range(8)], axis=0)
            hi, lo = split(w)
            wts[0:64, cols] = hi
            wts[64:128, cols] = lo
        span = slice(128 * g * group, 128 * (g + 1) * group)
        hi, lo = wts[0:64, span], wts[64:128, span]
        h = jnp.dot(field, jnp.concatenate([hi, hi, lo, lo], axis=0), preferred_element_type=F32)
        for t in range(g * group, g * group + group):
            cols = slice(128 * t, 128 * t + 128)
            sub = slice(128 * (t - g * group), 128 * (t - g * group) + 128)
            code = host_at(t)
            q = (code // 4) * 2 + code % 2
            drag = drag_at(t) * (-MASS)
            at = [q == i for i in range(4)]
            ones = [jnp.where(at[i], 1.0, 0.0) for i in range(4)]
            ones = [jnp.concatenate(ones[2 * x : 2 * x + 2], axis=0).astype(BF16) for x in range(2)]
            lines = [base[0:8, cols], base[8:16, cols]]
            carried = []
            for c in range(3):
                acc = None
                for a1 in range(2):
                    r = (a1 * 12 + c * 4) * 8
                    v = h[r : r + 8, sub]
                    for i in range(1, 4):
                        v = jnp.where(at[i], h[r + 8 * i : r + 8 * i + 8, sub], v)
                    v = v * lines[a1]
                    acc = v if acc is None else acc + v
                carried.append(jnp.sum(acc, axis=0, keepdims=True))
            emit(t, carried)
            speed = velocity_at(t)
            for c in range(3):
                r = drag * (carried[c] - speed[c])
                for a1 in range(2):
                    v = r * lines[a1]
                    hi = v.astype(BF16).astype(F32)
                    lo = v - hi
                    for part, value in enumerate((hi, lo)):
                        first = ((part * 2 + a1) * 3 + c) * 32
                        twice = jnp.concatenate([value, value], axis=0).astype(BF16)
                        ra[first : first + 16, cols] = twice * ones[0]
                        ra[first + 16 : first + 32, cols] = twice * ones[1]
        d = lax.dot_general(
            ra[:, span], wts[:, span], (((1,), (1,)), ((), ())), preferred_element_type=F32
        )
        total = d if total is None else total + d
    d = total[0:192] + total[192:384]
    d = d + pltpu.roll(d, 64, 1)
    return jnp.where(iota((96, 128), 1) < 64, d[0:96], d[96:192])


ALONG = ("drift", "drift", "cross", "cross")
FACES = 32
BACK = 16


def ups():
    odd_d, odd_c = parity("drift"), parity("cross")
    return odd_d, jnp.logical_not(odd_d), odd_c, jnp.logical_not(odd_c)


def towards(s, up):
    return 2 * (s // 2) + up.astype(jnp.int32)


def faces_to(s, up, packed):
    low, high = packed[2 * (s // 2) : 2 * (s // 2) + 2]
    return jnp.where(up, high, low)


def mark(lists, onehot):
    lane_row = iota((128, 128), 0)
    for t in range(16):
        low = lists[t : t + 1, :] & 127
        onehot[:, 128 * t : 128 * t + 128] = jnp.where(lane_row == low, 1.0, 0.0).astype(BF16)


def gather(s, hi_lo, lists, onehot, out):
    span = onehot[:, 512 * s : 512 * s + 512]
    y = jnp.dot(hi_lo, jnp.concatenate([span, span], axis=0), preferred_element_type=F32)
    for t in range(4):
        high = lists[4 * s + t : 4 * s + t + 1, :] >> 7
        g = jnp.zeros((8, 128), F32)
        for row in range(16):
            g = jnp.where(high == row, y[8 * row : 8 * row + 8, 128 * t : 128 * t + 128], g)
        out[8 * t : 8 * t + 8, :] = g


def send_kernel(
    fl, co, ve, dr, ho, mi, ta, la, o0, o1, o2, o3, vf, vc, vv, vd, vh, lists, vt, vl, onehot, vm, table, sems
):
    pairs = ((mi, vm), (co, vc), (ve, vv), (dr, vd), (ho, vh), (fl, vf), (ta, vt), (la, vl))
    copies = [pltpu.make_async_copy(src, dst, sems.at[n]) for n, (src, dst) in enumerate(pairs)]
    for copy in copies:
        copy.start()
    up = ups()
    copies[0].wait()
    for s in range(4):
        for t in range(4):
            lists[4 * s + t : 4 * s + t + 1, :] = vm[pl.ds(4 * t + towards(s, up[s]), 1), :]
    mark(lists, onehot)
    for copy in copies[1:]:
        copy.wait()
    for c in range(3):
        table[pl.ds(c, 16, stride=8), :] = vc[16 * c : 16 * c + 16, :]
        table[pl.ds(3 + c, 16, stride=8), :] = vv[16 * c : 16 * c + 16, :]
    table[pl.ds(6, 16, stride=8), :] = vd[...]
    table[pl.ds(7, 16, stride=8), :] = vh[...].astype(F32)
    parts = jnp.concatenate(split(table[...]), axis=1)
    packed = pack_faces(functools.partial(tile_of, vf))
    for s, out in enumerate((o0, o1, o2, o3)):
        out[FACES:, :] = faces_to(s, up[s], packed)
        gather(s, parts, lists, onehot, out)


def own_kernel(
    fl, co, ve, dr, ho, lists, tab, lane_op, onehot, dep_out, vel_out, base_out, operand_out, car, base, wts, ra
):
    sub16 = iota((16, 128), 0)
    rows = [jnp.where((lists[t : t + 1, :] >> 7) == sub16, 1.0, 0.0) for t in range(16)]
    rows = jnp.concatenate(rows, axis=1).astype(BF16)
    listed = lax.dot_general(rows, onehot[...], (((1,), (1,)), ((), ())), preferred_element_type=F32)
    own = jnp.where(listed > 0.5, 0.0, 1.0)
    get = functools.partial(tile_of, fl)
    field = field_operand(get)
    operand_out[...] = field
    drag_own = dr[...] * own

    def emit(t, carried):
        for c in range(3):
            car[16 * c + t : 16 * c + t + 1, :] = carried[c]

    dep_out[...] = couple(
        16,
        lambda t: [row_of(co, 16 * c + t) for c in range(3)],
        lambda t: [row_of(ve, 16 * c + t) for c in range(3)],
        lambda t: jnp.broadcast_to(drag_own[t : t + 1], (8, 128)),
        lambda t: row_of(ho, t),
        field, emit, base, wts, ra,
    )
    for c in range(3):
        r = slice(16 * c, 16 * c + 16)
        vel_out[r, :] = ve[r, :] + dr[...] * (car[r, :] * own - ve[r, :])
    out = local_step(get, tab, lane_op)
    for n, i in enumerate(CXZ):
        base_out[8 * n : 8 * n + 8, :] = out[i]


def host_lists(received, back, dep_in, operand, scratch):
    pick = lambda t, v: row_of(received[t // 4], 8 * (t % 4) + v)

    def emit(t, carried):
        rows = carried + [carried[0]]
        for c in range(4):
            back[t // 4][4 * (t % 4) + c : 4 * (t % 4) + c + 1, :] = rows[c]

    return dep_in[...] + couple(
        4 * len(received),
        lambda t: [pick(t, c) for c in range(3)],
        lambda t: [pick(t, 3 + c) for c in range(3)],
        lambda t: pick(t, 6),
        lambda t: pick(t, 7).astype(jnp.int32),
        operand[...], emit, *scratch,
    )


def near_kernel(r1, r3, operand, dep_in, dep_out, b1, b3, *scratch):
    dep_out[...] = host_lists((r1, r3), (b1, b3), dep_in, operand, scratch)


def far_kernel(r0, r1, r2, r3, operand, dep_in, base_in, b1, b3, u_out, dep_out, o0, o1, o2, o3, *scratch):
    dep = host_lists((r0, r2), (o0, o2), dep_in, operand, scratch)
    dep_out[...] = dep
    up = ups()
    parts = [face_part(ALONG[s], up[s], r[FACES:, :]) for s, r in enumerate((r0, r1, r2, r3))]
    new = {}
    for n, i in enumerate(CXZ):
        r = slice(8 * n, 8 * n + 8)
        new[i] = base_in[r, :] + sum(part(*i) for part in parts) + 0.5 * dep[r]
        u_out[r, :] = new[i]
    packed = pack_faces(lambda c, x, z: new[c, x, z])
    o1[0:BACK, :] = b1[...]
    o3[0:BACK, :] = b3[...]
    for s, out in enumerate((o0, o1, o2, o3)):
        out[BACK:, :] = faces_to(s, up[s], packed)


def second_kernel(u, dep, tab, lane_op, out_ref):
    out = local_step(functools.partial(tile_of, u), tab, lane_op)
    for n, i in enumerate(CXZ):
        r = slice(8 * n, 8 * n + 8)
        out_ref[r, :] = out[i] + 0.5 * dep[r, :]


def last_kernel(r0, r1, r2, r3, base, vel, dr, lists, onehot, fluid_out, vel_out):
    received = [r[...] for r in (r0, r1, r2, r3)]
    up = ups()
    parts = [face_part(ALONG[s], up[s], received[s][BACK:]) for s in range(4)]
    for n, i in enumerate(CXZ):
        fluid_out[8 * n : 8 * n + 8, :] = tile_of(base, *i) + sum(part(*i) for part in parts)
    sub16 = iota((16, 128), 0)
    columns = []
    for s in range(4):
        for t in range(4):
            at = (lists[4 * s + t : 4 * s + t + 1, :] >> 7) == sub16
            back = received[s][4 * t : 4 * t + 4]
            columns.append(jnp.concatenate([jnp.where(at, back[c : c + 1], 0.0) for c in range(3)], axis=0))
    rows = jnp.concatenate(split(jnp.concatenate(columns, axis=1)), axis=0)
    put = lax.dot_general(rows, onehot[...], (((1,), (1,)), ((), ())), preferred_element_type=F32)
    put = put[0:48] + put[48:96]
    for c in range(3):
        r = slice(16 * c, 16 * c + 16)
        vel_out[r, :] = vel[r, :] + dr[...] * put[r]


def shape(rows, dtype=F32, lanes=128):
    return jax.ShapeDtypeStruct((rows, lanes), dtype)


def call(kernel, outs, scratch=(), in_specs=None, cost=0, **kw):
    if in_specs is not None:
        kw["in_specs"] = in_specs
    return pl.pallas_call(
        kernel,
        out_shape=outs,
        scratch_shapes=list(scratch),
        cost_estimate=pl.CostEstimate(flops=cost, bytes_accessed=0, transcendentals=0),
        compiler_params=pltpu.CompilerParams(vmem_limit_bytes=VMEM),
        **kw,
    )


def exchange(messages):
    rows, columns = lax.axis_size("drift"), lax.axis_size("cross")

    def partner(i, j, s):
        if s < 2:
            return (i + (1 if i % 2 != s else -1)) % rows, j
        return i, (j + (1 if j % 2 != s - 2 else -1)) % columns

    received = []
    for n, message in enumerate(messages):
        pairs = []
        for i in range(rows):
            for j in range(columns):
                k, l = partner(i, j, n)
                pairs.append((i * columns + j, k * columns + l))
        received.append(lax.ppermute(message, ("drift", "cross"), pairs))
    return received


def per_device(fluid_field, coords, velocity, drag_factor, host_ids, migrants):
    field = fluid_field.reshape(3, 2, 2, 8, 128).transpose(0, 1, 3, 2, 4).reshape(96, 128)
    args = (
        field,
        coords.reshape(48, 128),
        velocity.reshape(48, 128),
        drag_factor.reshape(16, 128),
        host_ids.reshape(16, 128),
        migrants.reshape(4, 4, 128).transpose(1, 0, 2).reshape(16, 128),
    )
    args += tuple(jnp.asarray(t) for t in operator_tables())
    back = shape(BACK)

    def scratch(tiles):
        n = 128 * tiles
        return [pltpu.VMEM((16, n), F32), pltpu.VMEM((128, n), BF16), pltpu.VMEM((384, n), BF16)]

    outs = call(
        send_kernel,
        [shape(48)] * 4
        + [shape(a.shape[0], a.dtype, a.shape[1]) for a in args]
        + [shape(128, BF16, 2048)],
        [
            pltpu.VMEM((16, 128), jnp.int32),
            pltpu.VMEM((128, 128), F32),
            pltpu.SemaphoreType.DMA((8,)),
        ],
        in_specs=[pl.BlockSpec(memory_space=pl.ANY)] * 8,
    )(*(pltpu.with_memory_space_constraint(a, pltpu.HBM) for a in args))
    sends, args, onehot = outs[:4], outs[4:12], outs[12]
    drag, lists, tab, lane_op = args[3], *args[5:]
    r0, r1, r2, r3 = exchange(sends)
    dep, vel, base, operand = call(
        own_kernel,
        [shape(96), shape(48), shape(96), shape(192, BF16, 256)],
        [pltpu.VMEM((48, 128), F32)] + scratch(16),
        cost=1 << 31,
    )(*args, onehot)
    dep, *rest = call(near_kernel, [shape(96)] + [back] * 2, scratch(8), cost=1 << 30)(r1, r3, operand, dep)
    u, dep, *sends = call(far_kernel, [shape(96)] * 2 + [shape(32)] * 4, scratch(8))(
        r0, r1, r2, r3, operand, dep, base, *rest
    )
    received = exchange(sends)
    base = call(second_kernel, shape(96), cost=1 << 30)(u, dep, tab, lane_op)
    fluid, vel = call(last_kernel, [shape(96), shape(48)])(*received, base, vel, drag, lists, onehot)
    fluid = fluid.reshape(3, 2, 8, 2, 128).transpose(0, 1, 3, 2, 4).reshape(3, 2, 2, 1024)
    return fluid, vel.reshape(3, 1, 1, 2048)


def solution(mesh):
    field = P(None, "drift", "cross", None)
    scalar = P("drift", "cross", None)
    return jax.shard_map(
        per_device,
        mesh=mesh,
        in_specs=(field, field, field, scalar, scalar, P("drift", "cross", None, None)),
        out_specs=(field, field),
        check_vma=False,
    )
```

```python
import functools

import jax
import jax.numpy as jnp
import numpy as np
from jax import lax
from jax.experimental import pallas as pl
from jax.experimental.pallas import tpu as pltpu
from jax.sharding import PartitionSpec as P


F32 = jnp.float32
BF16 = jnp.bfloat16
MASS = 4.0
DIFF = 0.002
PEN = 0.05
VMEM = 24 << 20

NODES = -np.cos(np.pi * np.arange(8) / 7.0)
DENOM = np.array([np.prod([NODES[t] - NODES[m] for m in range(8) if m != t]) for t in range(8)])


def second_np():
    end = np.where((np.arange(8) == 0) | (np.arange(8) == 7), 2.0, 1.0)
    d = np.zeros((8, 8))
    for i in range(8):
        for m in range(8):
            if i != m:
                d[i, m] = end[i] / end[m] * (-1.0) ** (i + m) / (NODES[i] - NODES[m])
    d -= np.diag(d.sum(axis=1))
    return d @ d


def operator_tables():
    s = second_np()
    tab = np.zeros((2, 4, 8, 128))
    a1 = np.arange(128) // 64
    b = np.arange(128) // 8 % 8
    k = np.arange(128) % 8
    for sub in range(8):
        a2 = sub // 2
        a = 2 * a2 + a1
        for step in range(4):
            other = (a2 - step) % 4
            tab[0, step, sub] = DIFF * s[a, 2 * other + a1]
            tab[1, step, sub] = DIFF * s[a, 2 * other + 1 - a1]
        mult = ((a == 0) | (a == 7)) * 1.0 + ((b == 0) | (b == 7)) + ((k == 0) | (k == 7))
        tab[0, 0, sub] += 1.0 - PEN * mult
    eye = np.eye(8)
    side = DIFF * (np.kron(s, eye) + np.kron(eye, s))
    lane = np.kron(np.eye(2), side).T.astype(np.float32)
    hi = lane.astype(jnp.bfloat16)
    lo = (lane - hi.astype(np.float32)).astype(jnp.bfloat16)
    half = np.concatenate([hi, lo], axis=1)
    return tab.reshape(64, 128).astype(np.float32), np.concatenate([half, half], axis=0)


def iota(shape, dim):
    return lax.broadcasted_iota(jnp.int32, shape, dim)


def split(x):
    hi = x.astype(BF16)
    lo = (x - hi.astype(F32)).astype(BF16)
    return hi, lo


def row_of(ref, r):
    return jnp.broadcast_to(ref[r : r + 1, :], (8, 128))


def sublane_table(values):
    sub = iota((8, 128), 0)
    out = jnp.full((8, 128), float(values[0]), F32)
    for i in range(1, 8):
        out = jnp.where(sub == i, float(values[i]), out)
    return out


def node_tables(order):
    partners = [[m for m in range(8) if m != t] for t in order]
    tables = [sublane_table([NODES[p[j]] for p in partners]) for j in range(7)]
    return tables, sublane_table([1.0 / DENOM[t] for t in order])


def lagrange(s, tables):
    nodes, scale = tables
    out = (s - nodes[0]) * scale
    for t in nodes[1:]:
        out = out * (s - t)
    return out


def tile_of(ref, c, x, z):
    r = ((c * 2 + x) * 2 + z) * 8
    return ref[r : r + 8, :]


CXZ = [(c, x, z) for c in range(3) for x in range(2) for z in range(2)]


def parity(axis):
    return lax.rem(lax.axis_index(axis), 2) == 1


def face_masks():
    sub, lane = iota((8, 128), 0), iota((8, 128), 1)
    a2, y, a1, b, k = sub // 2, sub % 2, lane // 64, lane // 8 % 8, lane % 8
    pick = lambda cond: jnp.where(cond, PEN, 0.0).astype(F32)
    return dict(
        x_lo=pick((a2 == 0) & (a1 == 0)),
        x_hi=pick((a2 == 3) & (a1 == 1)),
        y_lo=pick((y == 0) & (b == 0)),
        y_hi=pick((y == 1) & (b == 7)),
        y_in_hi=pick((y == 0) & (b == 7)),
        y_in_lo=pick((y == 1) & (b == 0)),
        z_lo=pick(k == 0),
        z_hi=pick(k == 7),
    )


def pack_faces(get):
    lane = iota((8, 128), 1)
    b = lane // 8 % 8
    low = [get(c, 0, z)[0:2] for c in range(3) for z in range(2)]
    high = [get(c, 1, z)[6:8] for c in range(3) for z in range(2)]
    fill = jnp.zeros((4, 128), F32)
    x_lo = pltpu.roll(jnp.concatenate(low + [fill], axis=0), 64, 1)
    x_hi = pltpu.roll(jnp.concatenate(high + [fill], axis=0), 64, 1)
    y_lo, y_hi = [], []
    for group in range(2):
        lo = hi = None
        for i in range(6):
            v = get(*CXZ[group * 6 + i])
            here = b == i
            to_lo = v if i == 0 else pltpu.roll(v, 8 * i, 1)
            to_hi = pltpu.roll(v, (8 * i + 72) % 128, 1)
            lo = to_lo if lo is None else jnp.where(here, to_lo, lo)
            hi = to_hi if hi is None else jnp.where(here, to_hi, hi)
        y_lo.append(pltpu.roll(lo, 1, 0))
        y_hi.append(pltpu.roll(hi, 7, 0))
    return x_lo, x_hi, jnp.concatenate(y_lo, axis=0), jnp.concatenate(y_hi, axis=0)


def face_part(along, up, message):
    m = face_masks()
    if along == "drift":
        sides = (jnp.where(up, 0.0, m["x_lo"]), jnp.where(up, m["x_hi"], 0.0))

        def at(c, x, z):
            r = 2 * (c * 2 + z)
            return jnp.concatenate([message[r : r + 2]] * 4, axis=0) * sides[x]

        return at
    side = jnp.where(up, m["y_hi"], m["y_lo"])
    pieces = [message[8 * g : 8 * g + 8] for g in range(2)]
    pieces = [jnp.where(up, pltpu.roll(v, 56, 1), v) for v in pieces]

    def at(c, x, z):
        index = (c * 2 + x) * 2 + z
        g, i = index // 6, index % 6
        return (pltpu.roll(pieces[g], 128 - 8 * i, 1) if i else pieces[g]) * side

    return at


def local_step(get, tab, lane_op):
    m = face_masks()
    whole = jnp.concatenate([get(*i) for i in CXZ], axis=0)
    hi, lo = split(whole)
    product = jnp.dot(jnp.concatenate([hi, lo], axis=1), lane_op[...], preferred_element_type=F32)
    product = product[:, 0:128] + product[:, 128:256]
    turned = {}
    for i in CXZ:
        v = get(*i)
        w = pltpu.roll(v, 64, 1)
        turned[i] = (
            [v] + [pltpu.roll(v, 2 * s, 0) for s in range(1, 4)],
            [w] + [pltpu.roll(w, 2 * s, 0) for s in range(1, 4)],
        )
    out = {}
    for n, (c, x, z) in enumerate(CXZ):
        v = turned[c, x, z][0][0]
        total = product[8 * n : 8 * n + 8]
        for kind in range(2):
            for s in range(4):
                r = (kind * 4 + s) * 8
                total = total + turned[c, x, z][kind][s] * tab[r : r + 8, :]
        beside = turned[c, 1 - x, z][1]
        total = total + (beside[3] * m["x_hi"] if x == 0 else beside[1] * m["x_lo"])
        total = total + pltpu.roll(pltpu.roll(v, 56, 1), 7, 0) * m["y_in_hi"]
        total = total + pltpu.roll(pltpu.roll(v, 72, 1), 1, 0) * m["y_in_lo"]
        across = turned[c, x, 1 - z][0][0]
        if z == 0:
            total = total + pltpu.roll(across, 7, 1) * m["z_hi"]
        else:
            total = total + pltpu.roll(across, 121, 1) * m["z_lo"]
        out[c, x, z] = total
    return out


def field_operand(get):
    lane = iota((96, 128), 1)
    whole = jnp.concatenate([get(*i) for i in CXZ], axis=0)
    hi = whole.astype(BF16).astype(F32)
    lo = whole - hi
    first = jnp.where(lane < 64, hi, pltpu.roll(lo, 64, 1)).astype(BF16)
    second = jnp.where(lane < 64, pltpu.roll(hi, 64, 1), lo).astype(BF16)
    rows = jnp.concatenate([first, second], axis=0)
    return jnp.concatenate([rows, rows], axis=1)


def couple(n_tiles, coords_at, velocity_at, drag_at, host_at, field, emit, base, wts, ra, group=8):
    even = node_tables([0, 0, 2, 2, 4, 4, 6, 6])
    odd = node_tables([1, 1, 3, 3, 5, 5, 7, 7])
    plain = node_tables(list(range(8)))
    y_sub = iota((8, 128), 0) % 2
    total = None
    for g in range(n_tiles // group):
        for t in range(g * group, g * group + group):
            cols = slice(128 * t, 128 * t + 128)
            sx, sy, sz = coords_at(t)
            y_of = (host_at(t) // 2) % 2
            keep = y_of == y_sub
            base[0:8, cols] = jnp.where(keep, lagrange(sx, even), 0.0)
            base[8:16, cols] = jnp.where(keep, lagrange(sx, odd), 0.0)
            lb, lc = lagrange(sy, plain), lagrange(sz, plain)
            w = jnp.concatenate([jnp.broadcast_to(lb[b : b + 1], (8, 128)) * lc for b in range(8)], axis=0)
            hi, lo = split(w)
            wts[0:64, cols] = hi
            wts[64:128, cols] = lo
        span = slice(128 * g * group, 128 * (g + 1) * group)
        hi, lo = wts[0:64, span], wts[64:128, span]
        h = jnp.dot(field, jnp.concatenate([hi, hi, lo, lo], axis=0), preferred_element_type=F32)
        for t in range(g * group, g * group + group):
            cols = slice(128 * t, 128 * t + 128)
            sub = slice(128 * (t - g * group), 128 * (t - g * group) + 128)
            code = host_at(t)
            q = (code // 4) * 2 + code % 2
            drag = drag_at(t) * (-MASS)
            at = [q == i for i in range(4)]
            ones = [jnp.where(at[i], 1.0, 0.0) for i in range(4)]
            ones = [jnp.concatenate(ones[2 * x : 2 * x + 2], axis=0).astype(BF16) for x in range(2)]
            lines = [base[0:8, cols], base[8:16, cols]]
            carried = []
            for c in range(3):
                acc = None
                for a1 in range(2):
                    r = (a1 * 12 + c * 4) * 8
                    v = h[r : r + 8, sub]
                    for i in range(1, 4):
                        v = jnp.where(at[i], h[r + 8 * i : r + 8 * i + 8, sub], v)
                    v = v * lines[a1]
                    acc = v if acc is None else acc + v
                carried.append(jnp.sum(acc, axis=0, keepdims=True))
            emit(t, carried)
            speed = velocity_at(t)
            for c in range(3):
                r = drag * (carried[c] - speed[c])
                for a1 in range(2):
                    v = r * lines[a1]
                    hi = v.astype(BF16).astype(F32)
                    lo = v - hi
                    for part, value in enumerate((hi, lo)):
                        first = ((part * 2 + a1) * 3 + c) * 32
                        twice = jnp.concatenate([value, value], axis=0).astype(BF16)
                        ra[first : first + 16, cols] = twice * ones[0]
                        ra[first + 16 : first + 32, cols] = twice * ones[1]
        d = lax.dot_general(
            ra[:, span], wts[:, span], (((1,), (1,)), ((), ())), preferred_element_type=F32
        )
        total = d if total is None else total + d
    d = total[0:192] + total[192:384]
    d = d + pltpu.roll(d, 64, 1)
    return jnp.where(iota((96, 128), 1) < 64, d[0:96], d[96:192])


ALONG = ("drift", "drift", "cross", "cross")
FACES = 32
BACK = 16


def ups():
    odd_d, odd_c = parity("drift"), parity("cross")
    return odd_d, jnp.logical_not(odd_d), odd_c, jnp.logical_not(odd_c)


def towards(s, up):
    return 2 * (s // 2) + up.astype(jnp.int32)


def faces_to(s, up, packed):
    low, high = packed[2 * (s // 2) : 2 * (s // 2) + 2]
    return jnp.where(up, high, low)


def mark(lists, onehot):
    lane_row = iota((128, 128), 0)
    for t in range(16):
        low = lists[t : t + 1, :] & 127
        onehot[:, 128 * t : 128 * t + 128] = jnp.where(lane_row == low, 1.0, 0.0).astype(BF16)


def gather(s, hi_lo, lists, onehot, out):
    span = onehot[:, 512 * s : 512 * s + 512]
    y = jnp.dot(hi_lo, jnp.concatenate([span, span], axis=0), preferred_element_type=F32)
    for t in range(4):
        high = lists[4 * s + t : 4 * s + t + 1, :] >> 7
        g = jnp.zeros((8, 128), F32)
        for row in range(16):
            g = jnp.where(high == row, y[8 * row : 8 * row + 8, 128 * t : 128 * t + 128], g)
        out[8 * t : 8 * t + 8, :] = g


def send_kernel(
    fl, co, ve, dr, ho, mi, ta, la, o0, o1, o2, o3, vf, vc, vv, vd, vh, lists, vt, vl, onehot, vm, table, sems
):
    pairs = ((mi, vm), (co, vc), (ve, vv), (dr, vd), (ho, vh), (fl, vf), (ta, vt), (la, vl))
    copies = [pltpu.make_async_copy(src, dst, sems.at[n]) for n, (src, dst) in enumerate(pairs)]
    for copy in copies:
        copy.start()
    up = ups()
    copies[0].wait()
    for s in range(4):
        for t in range(4):
            lists[4 * s + t : 4 * s + t + 1, :] = vm[pl.ds(4 * t + towards(s, up[s]), 1), :]
    mark(lists, onehot)
    for copy in copies[1:6]:
        copy.wait()
    for c in range(3):
        table[pl.ds(c, 16, stride=8), :] = vc[16 * c : 16 * c + 16, :]
        table[pl.ds(3 + c, 16, stride=8), :] = vv[16 * c : 16 * c + 16, :]
    table[pl.ds(6, 16, stride=8), :] = vd[...]
    table[pl.ds(7, 16, stride=8), :] = vh[...].astype(F32)
    parts = jnp.concatenate(split(table[...]), axis=1)
    packed = pack_faces(functools.partial(tile_of, vf))
    for s, out in enumerate((o0, o1, o2, o3)):
        out[FACES:, :] = faces_to(s, up[s], packed)
        gather(s, parts, lists, onehot, out)
    for copy in copies[6:]:
        copy.wait()


def own_kernel(
    fl, co, ve, dr, ho, lists, tab, lane_op, onehot, dep_out, vel_out, base_out, operand_out, car, base, wts, ra
):
    sub16 = iota((16, 128), 0)
    rows = [jnp.where((lists[t : t + 1, :] >> 7) == sub16, 1.0, 0.0) for t in range(16)]
    rows = jnp.concatenate(rows, axis=1).astype(BF16)
    listed = lax.dot_general(rows, onehot[...], (((1,), (1,)), ((), ())), preferred_element_type=F32)
    own = jnp.where(listed > 0.5, 0.0, 1.0)
    get = functools.partial(tile_of, fl)
    field = field_operand(get)
    operand_out[...] = field
    drag_own = dr[...] * own

    def emit(t, carried):
        for c in range(3):
            car[16 * c + t : 16 * c + t + 1, :] = carried[c]

    dep_out[...] = couple(
        16,
        lambda t: [row_of(co, 16 * c + t) for c in range(3)],
        lambda t: [row_of(ve, 16 * c + t) for c in range(3)],
        lambda t: jnp.broadcast_to(drag_own[t : t + 1], (8, 128)),
        lambda t: row_of(ho, t),
        field, emit, base, wts, ra,
    )
    for c in range(3):
        r = slice(16 * c, 16 * c + 16)
        vel_out[r, :] = ve[r, :] + dr[...] * (car[r, :] * own - ve[r, :])
    out = local_step(get, tab, lane_op)
    for n, i in enumerate(CXZ):
        base_out[8 * n : 8 * n + 8, :] = out[i]


def host_lists(received, back, dep_in, operand, scratch):
    pick = lambda t, v: row_of(received[t // 4], 8 * (t % 4) + v)

    def emit(t, carried):
        rows = carried + [carried[0]]
        for c in range(4):
            back[t // 4][4 * (t % 4) + c : 4 * (t % 4) + c + 1, :] = rows[c]

    return dep_in[...] + couple(
        4 * len(received),
        lambda t: [pick(t, c) for c in range(3)],
        lambda t: [pick(t, 3 + c) for c in range(3)],
        lambda t: pick(t, 6),
        lambda t: pick(t, 7).astype(jnp.int32),
        operand[...], emit, *scratch,
    )


def near_kernel(r1, r3, operand, dep_in, dep_out, b1, b3, *scratch):
    dep_out[...] = host_lists((r1, r3), (b1, b3), dep_in, operand, scratch)


def far_kernel(r0, r1, r2, r3, operand, dep_in, base_in, b1, b3, u_out, dep_out, o0, o1, o2, o3, *scratch):
    dep = host_lists((r0, r2), (o0, o2), dep_in, operand, scratch)
    dep_out[...] = dep
    up = ups()
    parts = [face_part(ALONG[s], up[s], r[FACES:, :]) for s, r in enumerate((r0, r1, r2, r3))]
    new = {}
    for n, i in enumerate(CXZ):
        r = slice(8 * n, 8 * n + 8)
        new[i] = base_in[r, :] + sum(part(*i) for part in parts) + 0.5 * dep[r]
        u_out[r, :] = new[i]
    packed = pack_faces(lambda c, x, z: new[c, x, z])
    o1[0:BACK, :] = b1[...]
    o3[0:BACK, :] = b3[...]
    for s, out in enumerate((o0, o1, o2, o3)):
        out[BACK:, :] = faces_to(s, up[s], packed)


def second_kernel(u, dep, tab, lane_op, out_ref):
    out = local_step(functools.partial(tile_of, u), tab, lane_op)
    for n, i in enumerate(CXZ):
        r = slice(8 * n, 8 * n + 8)
        out_ref[r, :] = out[i] + 0.5 * dep[r, :]


def last_kernel(r0, r1, r2, r3, base, vel, dr, lists, onehot, fluid_out, vel_out):
    received = [r[...] for r in (r0, r1, r2, r3)]
    up = ups()
    parts = [face_part(ALONG[s], up[s], received[s][BACK:]) for s in range(4)]
    for n, i in enumerate(CXZ):
        fluid_out[8 * n : 8 * n + 8, :] = tile_of(base, *i) + sum(part(*i) for part in parts)
    sub16 = iota((16, 128), 0)
    columns = []
    for s in range(4):
        for t in range(4):
            at = (lists[4 * s + t : 4 * s + t + 1, :] >> 7) == sub16
            back = received[s][4 * t : 4 * t + 4]
            columns.append(jnp.concatenate([jnp.where(at, back[c : c + 1], 0.0) for c in range(3)], axis=0))
    rows = jnp.concatenate(split(jnp.concatenate(columns, axis=1)), axis=0)
    put = lax.dot_general(rows, onehot[...], (((1,), (1,)), ((), ())), preferred_element_type=F32)
    put = put[0:48] + put[48:96]
    for c in range(3):
        r = slice(16 * c, 16 * c + 16)
        vel_out[r, :] = vel[r, :] + dr[...] * put[r]


def shape(rows, dtype=F32, lanes=128):
    return jax.ShapeDtypeStruct((rows, lanes), dtype)


def call(kernel, outs, scratch=(), in_specs=None, cost=0, **kw):
    if in_specs is not None:
        kw["in_specs"] = in_specs
    return pl.pallas_call(
        kernel,
        out_shape=outs,
        scratch_shapes=list(scratch),
        cost_estimate=pl.CostEstimate(flops=cost, bytes_accessed=0, transcendentals=0),
        compiler_params=pltpu.CompilerParams(vmem_limit_bytes=VMEM),
        **kw,
    )


def exchange(messages):
    rows, columns = lax.axis_size("drift"), lax.axis_size("cross")

    def partner(i, j, s):
        if s < 2:
            return (i + (1 if i % 2 != s else -1)) % rows, j
        return i, (j + (1 if j % 2 != s - 2 else -1)) % columns

    received = []
    for n, message in enumerate(messages):
        pairs = []
        for i in range(rows):
            for j in range(columns):
                k, l = partner(i, j, n)
                pairs.append((i * columns + j, k * columns + l))
        received.append(lax.ppermute(message, ("drift", "cross"), pairs))
    return received


def per_device(fluid_field, coords, velocity, drag_factor, host_ids, migrants):
    field = fluid_field.reshape(3, 2, 2, 8, 128).transpose(0, 1, 3, 2, 4).reshape(96, 128)
    args = (
        field,
        coords.reshape(48, 128),
        velocity.reshape(48, 128),
        drag_factor.reshape(16, 128),
        host_ids.reshape(16, 128),
        migrants.reshape(4, 4, 128).transpose(1, 0, 2).reshape(16, 128),
    )
    args += tuple(jnp.asarray(t) for t in operator_tables())
    back = shape(BACK)

    def scratch(tiles):
        n = 128 * tiles
        return [pltpu.VMEM((16, n), F32), pltpu.VMEM((128, n), BF16), pltpu.VMEM((384, n), BF16)]

    outs = call(
        send_kernel,
        [shape(48)] * 4
        + [shape(a.shape[0], a.dtype, a.shape[1]) for a in args]
        + [shape(128, BF16, 2048)],
        [
            pltpu.VMEM((16, 128), jnp.int32),
            pltpu.VMEM((128, 128), F32),
            pltpu.SemaphoreType.DMA((8,)),
        ],
        in_specs=[pl.BlockSpec(memory_space=pl.ANY)] * 8,
    )(*(pltpu.with_memory_space_constraint(a, pltpu.HBM) for a in args))
    sends, args, onehot = outs[:4], outs[4:12], outs[12]
    drag, lists, tab, lane_op = args[3], *args[5:]
    r0, r1, r2, r3 = exchange(sends)
    dep, vel, base, operand = call(
        own_kernel,
        [shape(96), shape(48), shape(96), shape(192, BF16, 256)],
        [pltpu.VMEM((48, 128), F32)] + scratch(16),
        cost=1 << 31,
    )(*args, onehot)
    dep, *rest = call(near_kernel, [shape(96)] + [back] * 2, scratch(8), cost=1 << 30)(r1, r3, operand, dep)
    u, dep, *sends = call(far_kernel, [shape(96)] * 2 + [shape(32)] * 4, scratch(8))(
        r0, r1, r2, r3, operand, dep, base, *rest
    )
    received = exchange(sends)
    base = call(second_kernel, shape(96), cost=1 << 30)(u, dep, tab, lane_op)
    fluid, vel = call(last_kernel, [shape(96), shape(48)])(*received, base, vel, drag, lists, onehot)
    fluid = fluid.reshape(3, 2, 8, 2, 128).transpose(0, 1, 3, 2, 4).reshape(3, 2, 2, 1024)
    return fluid, vel.reshape(3, 1, 1, 2048)


def solution(mesh):
    field = P(None, "drift", "cross", None)
    scalar = P("drift", "cross", None)
    return jax.shard_map(
        per_device,
        mesh=mesh,
        in_specs=(field, field, field, scalar, scalar, P("drift", "cross", None, None)),
        out_specs=(field, field),
        check_vma=False,
    )
```
